256 devices in a mesh: tm: 16 (over x, z_lo, core), lat: 16 (over z_hi, y).
Axes of the slice: x: 4, y: 4, z: 8 (z_hi: 4, z_lo: 2; z = z_hi * 2 + z_lo), core: 2. Of those that a mesh axis runs over, the one named last changes fastest.
Arguments:
- states: float32 [128, 1024, 256], P('tm', 'lat'), may hold values from -6 to 6
- multipliers: float32 [128, 1024, 256], P('tm', 'lat'), may hold values from -3 to 3
- diffusivity: float32 [1024, 256], P('lat'), may hold values from 0.02 to 0.15
- zonal_speed: float32 [1024, 256], P('lat'), may hold values from -0.3 to 0.3
- meridional_speed: float32 [1024, 256], P('lat'), may hold values from -0.3 to 0.3
- observed_cells: int32 [128, 16, 1024], P('tm', 'lat'), may hold values from 0 to 16383
- observed_values: float32 [128, 16, 1024], P('tm', 'lat'), may hold values from -6 to 6
- observed_weights: float32 [128, 16, 1024], P('tm', 'lat'), may hold values from 0.2 to 2
- fresh_cells: int32 [4, 16, 1024], P(None, 'lat'), may hold values from 0 to 16383
- fresh_values: float32 [4, 16, 1024], P(None, 'lat'), may hold values from -6 to 6
- fresh_weights: float32 [4, 16, 1024], P(None, 'lat'), may hold values from 0.2 to 2
Outputs:
- analysis: float32 [128, 1024, 256], P('tm', 'lat')
- lagrange: float32 [128, 1024, 256], P('tm', 'lat')
The draws below stay inside these ranges and needn't reach their ends.
Inputs may be any that keep to these rules, and one draw needn't show every extreme that they name: `observed_cells`: each entry names a cell of its band, counted row by row over the band's 64 x 256 cells; cells may repeat. `fresh_cells`: each entry names a cell of its band, counted row by row over the band's 64 x 256 cells; cells may repeat.
All inputs are finite; a program needn't handle non-finite values.
Results may differ from the reference program's by a relative error of at most 0.000059.
Values sent between devices are 32-bit elements; how exact they have to be, the bound alone decides.
A program may use at most 64 MiB of HBM per device.

```python
import math
import jax
import jax.numpy as jnp

ROWS = 64
LON = 256
NOBS = 1024
SWEEPS = 2
HALF = 4
TIMES = 128
NLAT = 1024
N_LAT = 16


def place_ends(array, own_key, smallest, top_value):
    spot = [jax.random.randint(jax.random.fold_in(own_key, axis), (), 0, length) for axis, length in enumerate(array.shape)]
    main_axis = array.shape.index(max(array.shape))
    neighbour = spot[:main_axis] + [(spot[main_axis] + 1) % array.shape[main_axis]] + spot[main_axis + 1:]
    return array.at[tuple(spot)].set(smallest).at[tuple(neighbour)].set(top_value)


def level_of(rng, extent, cuts, least, largest):
    def one(axis_at, parts):
        steps = jax.random.uniform(jax.random.fold_in(jax.random.fold_in(rng, 6), axis_at), (parts,), jnp.float32, least / len(cuts), largest / len(cuts))
        return jnp.repeat(jnp.exp(steps), extent[axis_at] // parts).reshape((-1,) + (1,) * (len(extent) - axis_at - 1))

    factor_of = one(*cuts[0])
    for cut in cuts[1:]:
        factor_of = factor_of * one(*cut)
    return factor_of


def centred(key, extent, scale, limit, pieces=(), kind=jnp.bfloat16):
    values = jax.random.normal(key, extent, jnp.float32) * scale
    if len(pieces) > 0:
        values = level_of(key, extent, pieces, -0.22, 0.18) * values
    return jnp.clip(values, min=-limit, max=limit).astype(kind)


def setup_inputs(seed: int = 0) -> dict:
    key_list = jax.random.split(jax.random.key(seed), 12)
    return {
        "states": centred(key_list[0], (TIMES, NLAT, LON), 1.0, 6.0, ((0, 16), (1, 16)), jnp.float32),
        "multipliers": centred(key_list[1], (TIMES, NLAT, LON), 0.5, 3.0, ((0, 16), (1, 16)), jnp.float32),
        "diffusivity": jnp.clip(0.02 + 0.13000001 * jax.random.uniform(key_list[2], (NLAT, LON), jnp.float32) ** level_of(key_list[2], (NLAT, LON), ((0, 16),), -0.2, 0.2), 0.02, 0.15),
        "zonal_speed": jnp.clip(jax.random.uniform(key_list[3], (NLAT, LON), jnp.float32, -0.3, 0.3) * level_of(key_list[3], (NLAT, LON), ((0, 16),), -0.4, 0.0), -0.3, 0.3),
        "meridional_speed": jnp.clip(jax.random.uniform(key_list[4], (NLAT, LON), jnp.float32, -0.3, 0.3) * level_of(key_list[4], (NLAT, LON), ((0, 16),), -0.4, 0.0), -0.3, 0.3),
        "observed_cells": place_ends(jax.random.randint(key_list[5], (TIMES, N_LAT, NOBS), 0, ROWS * LON), jax.random.fold_in(key_list[5], 1), 0, (ROWS * LON) - 1).astype(jnp.int32),
        "observed_values": centred(key_list[6], (TIMES, N_LAT, NOBS), 1.0, 6.0, ((0, 16), (1, 16)), jnp.float32),
        "observed_weights": jnp.clip(jnp.exp(math.log(2.0) - 2.3025851 * jax.random.uniform(key_list[7], (TIMES, N_LAT, NOBS), jnp.float32) ** level_of(key_list[7], (TIMES, N_LAT, NOBS), ((0, 16), (1, 16)), -0.2, 0.2)), 0.2, 2.0),
        "fresh_cells": place_ends(jax.random.randint(key_list[8], (HALF, N_LAT, NOBS), 0, ROWS * LON), jax.random.fold_in(key_list[8], 1), 0, (ROWS * LON) - 1).astype(jnp.int32),
        "fresh_values": centred(key_list[9], (HALF, N_LAT, NOBS), 1.0, 6.0, ((1, 16),), jnp.float32),
        "fresh_weights": jnp.clip(jnp.exp(math.log(2.0) - 2.3025851 * jax.random.uniform(key_list[10], (HALF, N_LAT, NOBS), jnp.float32) ** level_of(key_list[10], (HALF, N_LAT, NOBS), ((1, 16),), -0.2, 0.2)), 0.2, 2.0),
    }


penalty_weight = 1.0
step_size = 0.15


def pad_rows(field):
    widths = [(0, 0)] * (field.ndim - 2) + [(1, 1), (0, 0)]
    padded = jnp.pad(field, widths)
    return padded[..., 2:, :], padded[..., :-2, :]


def substep_forward(field, diffusivity, zonal_speed, meridional_speed):
    north_cells, south_cells = pad_rows(field)
    east_cells = jnp.roll(field, -1, axis=-1)
    west_cells = jnp.roll(field, 1, axis=-1)
    return (field + diffusivity * (north_cells + south_cells + east_cells + west_cells - 4.0 * field)
            - 0.5 * zonal_speed * (east_cells - west_cells) - 0.5 * meridional_speed * (north_cells - south_cells))


def substep_adjoint(field, diffusivity, zonal_speed, meridional_speed):
    spread = diffusivity * field
    carried = 0.5 * zonal_speed * field
    lifted = 0.5 * meridional_speed * field
    spread_north, spread_south = pad_rows(spread)
    lifted_north, lifted_south = pad_rows(lifted)
    return (field + spread_north + spread_south + jnp.roll(spread, -1, axis=-1) + jnp.roll(spread, 1, axis=-1)
            - 4.0 * spread - jnp.roll(carried, 1, axis=-1) + jnp.roll(carried, -1, axis=-1)
            - lifted_south + lifted_north)


def reference(states, multipliers, diffusivity, zonal_speed, meridional_speed,
              observed_cells, observed_values, observed_weights, fresh_cells, fresh_values, fresh_weights):
    def forward(field):
        for substep in range(3):
            field = substep_forward(field, diffusivity, zonal_speed, meridional_speed)
        return field

    def backward(field):
        for substep in range(3):
            field = substep_adjoint(field, diffusivity, zonal_speed, meridional_speed)
        return field

    time_index = jnp.arange(TIMES, dtype=jnp.int32)[:, None, None]
    band_index = jnp.arange(N_LAT, dtype=jnp.int32)[None, :, None]

    def sweep(field, lagrange, prior, cells, values, weights):
        if prior is None:
            head = field[:1]
        else:
            head = prior[None]
        predicted = jnp.concatenate([head, forward(field[:-1])], axis=0)
        jumps = field - predicted
        flat = field.reshape(TIMES, N_LAT, ROWS * LON)
        misfit = weights * (jnp.take_along_axis(flat, cells, axis=2) - values)
        pulled_back = jnp.zeros_like(flat).at[time_index, band_index, cells].add(misfit).reshape(field.shape)
        pulled = lagrange + penalty_weight * jumps
        following = jnp.concatenate([pulled[1:], jnp.zeros_like(pulled[:1])], axis=0)
        gradient = pulled_back + pulled - backward(following)
        return field - step_size * gradient, lagrange + penalty_weight * jumps

    field, lagrange = states, multipliers
    cells, values, weights = observed_cells, observed_values, observed_weights
    for repeat in range(SWEEPS):
        field, lagrange = sweep(field, lagrange, None, cells, values, weights)
    next_prior = forward(field[HALF - 1])
    tail = jnp.broadcast_to(field[-1:], (HALF, NLAT, LON))
    field = jnp.concatenate([field[HALF:], tail], axis=0)
    lagrange = jnp.concatenate([lagrange[HALF:], jnp.zeros_like(lagrange[:HALF])], axis=0)
    cells = jnp.concatenate([cells[HALF:], fresh_cells], axis=0)
    values = jnp.concatenate([values[HALF:], fresh_values], axis=0)
    weights = jnp.concatenate([weights[HALF:], fresh_weights], axis=0)
    for repeat in range(SWEEPS):
        field, lagrange = sweep(field, lagrange, next_prior, cells, values, weights)
    return field, lagrange
```

```python
import functools

import jax
import jax.numpy as jnp
from jax import lax
from jax.experimental import pallas as pl
from jax.experimental.pallas import tpu as pltpu
from jax.sharding import PartitionSpec as P

MESH = pl.DeviceIdType.MESH
STEP = 0.15
F32 = jnp.float32


def weave(n_tm, n_lat, n_transfers, *refs):
    (
        states,
        mults,
        diff,
        zonal,
        merid,
        cells,
        values,
        weights,
        f_cells,
        f_values,
        f_weights,
        x_out,
        l_out,
        XF,
        LF,
        T1,
        T2,
        CF,
        CB,
        ND,
        NF,
        NB,
        WF,
        VF,
        HX,
        HL,
        E,
        NX,
        NL,
        S7,
        S0,
        SL0,
        PKX,
        PKL,
        SL4,
        RKX,
        RKL,
        OC,
        OV,
        OW,
        ssem,
        rsem,
    ) = refs
    lon = 2 * XF.shape[-1]
    half_lon = lon // 2
    tm = lax.axis_index("tm")
    lat = lax.axis_index("lat")
    made = [0]

    def inside(dt, dl):
        ok = True
        if dt > 0:
            ok = tm < n_tm - 1
        elif dt < 0:
            ok = tm > 0
        if dl > 0:
            ok = jnp.logical_and(ok, lat < n_lat - 1)
        elif dl < 0:
            ok = jnp.logical_and(ok, lat > 0)
        return ok

    class Move:
        def __init__(self, src, dst, dt, dl):
            i = made[0]
            made[0] += 1
            assert i < n_transfers
            self.to, self.by = inside(dt, dl), inside(-dt, -dl)
            self.copy = pltpu.make_async_remote_copy(
                src_ref=src,
                dst_ref=dst,
                send_sem=ssem.at[i],
                recv_sem=rsem.at[i],
                device_id=(tm + dt, lat + dl),
                device_id_type=MESH,
            )
            pl.when(self.to)(self.copy.start)

        def finish(self):
            pl.when(self.to)(self.copy.wait_send)
            pl.when(self.by)(self.copy.wait_recv)

    barrier = pltpu.get_barrier_semaphore()
    greeted = 0
    for dt in (-1, 0, 1):
        for dl in (-1, 0, 1):
            if dt == 0 and dl == 0:
                continue
            ok = inside(dt, dl)

            @pl.when(ok)
            def _():
                pl.semaphore_signal(
                    barrier, inc=1, device_id=(tm + dt, lat + dl), device_id_type=MESH
                )

            greeted = greeted + ok.astype(jnp.int32)

    whole = slice(None)

    def blank(ref, *at):
        ref[at] = jnp.zeros(ref.at[at].shape, ref.dtype)

    @pl.when(lat == 0)
    def _():
        for r in range(4):
            blank(E, r, whole, slice(0, 8))
            blank(NX, r, whole, slice(0, 8))
        for k in range(3):
            blank(ND, k, whole, slice(0, 8))
        blank(NL, 0, whole, slice(0, 8))
        blank(XF, whole, slice(0, 48))
        blank(LF, whole, slice(0, 24))
        blank(RKX, whole, slice(0, 24))

    @pl.when(lat == n_lat - 1)
    def _():
        for r in range(4):
            blank(E, r, whole, slice(72, 80))
            blank(NX, r, whole, slice(72, 80))
        for k in range(3):
            blank(ND, k, whole, slice(72, 80))
        blank(NL, 0, whole, slice(72, 80))
        blank(XF, whole, slice(560, 608))
        blank(LF, whole, slice(536, 560))
        blank(RKX, whole, slice(280, 304))

    @pl.when(tm == 0)
    def _():
        blank(E, 0)
        blank(E, 1)

    @pl.when(tm == n_tm - 1)
    def _():
        for r in range(4):
            blank(NX, r)
        blank(NL, 0)
        blank(NL, 1)

    blank(XF, whole, slice(608, 640))
    blank(LF, whole, slice(560, 576))

    def split(x):
        return jnp.stack([x[:, :half_lon], x[:, half_lon:]])

    def join(x):
        return jnp.concatenate([x[0], x[1]], axis=1)

    for s in range(8):
        XF[:, pl.ds(48 + s, 64, stride=8), :] = split(states[s])
        LF[:, pl.ds(24 + s, 64, stride=8), :] = split(mults[s])
    S7[0] = split(states[7])
    S0[0] = split(states[0])
    SL0[...] = split(mults[0])
    for k, ref in enumerate((diff, zonal, merid)):
        ND[k, :, pl.ds(8, 64), :] = split(ref[...])

    pl.semaphore_wait(barrier, greeted)

    def send_after(r):
        return [
            Move(S0.at[r], NX.at[r, :, pl.ds(8, 64)], -1, 0),
            Move(S0.at[r, :, pl.ds(0, 8)], NX.at[r, :, pl.ds(72, 8)], -1, -1),
            Move(S0.at[r, :, pl.ds(56, 8)], NX.at[r, :, pl.ds(0, 8)], -1, 1),
        ]

    def send_before(r):
        return [
            Move(S7.at[r], E.at[r, :, pl.ds(8, 64)], 1, 0),
            Move(S7.at[r, :, pl.ds(0, 8)], E.at[r, :, pl.ds(72, 8)], 1, -1),
            Move(S7.at[r, :, pl.ds(56, 8)], E.at[r, :, pl.ds(0, 8)], 1, 1),
        ]

    def send_rows(r):
        return [
            Move(XF.at[:, pl.ds(48, 48)], HX.at[r, 1], 0, -1),
            Move(XF.at[:, pl.ds(512, 48)], HX.at[r, 0], 0, 1),
        ]

    def finish(moves):
        for move in moves:
            move.finish()

    def take_rows(r):
        @pl.when(lat > 0)
        def _():
            XF[:, pl.ds(0, 48), :] = HX[r, 0]

        @pl.when(lat < n_lat - 1)
        def _():
            XF[:, pl.ds(560, 48), :] = HX[r, 1]

    def edges(r):
        S7[r] = XF[:, pl.ds(55, 64, stride=8), :]
        S0[r] = XF[:, pl.ds(48, 64, stride=8), :]

    moves = send_rows(0)
    moves += [
        Move(LF.at[:, pl.ds(24, 24)], HL.at[1], 0, -1),
        Move(LF.at[:, pl.ds(512, 24)], HL.at[0], 0, 1),
    ]
    moves += [
        Move(ND.at[:, :, pl.ds(8, 8)], ND.at[:, :, pl.ds(72, 8)], 0, -1),
        Move(ND.at[:, :, pl.ds(64, 8)], ND.at[:, :, pl.ds(0, 8)], 0, 1),
    ]
    moves += send_before(0) + send_after(0)
    moves += [
        Move(SL0, NL.at[0, :, pl.ds(8, 64)], -1, 0),
        Move(SL0.at[:, pl.ds(0, 8)], NL.at[0, :, pl.ds(72, 8)], -1, -1),
        Move(SL0.at[:, pl.ds(56, 8)], NL.at[0, :, pl.ds(0, 8)], -1, 1),
    ]
    obs_moves = [
        Move(cells.at[pl.ds(0, 4)], OC, -1, 0),
        Move(values.at[pl.ds(0, 4)], OV, -1, 0),
        Move(weights.at[pl.ds(0, 4)], OW, -1, 0),
    ]

    n_obs = cells.shape[-1]

    def tables(c, y, w):
        row = lax.shift_right_logical(c, 8)
        column = lax.bitwise_and(c, 255)
        on_row = lax.broadcasted_iota(jnp.int32, (64, n_obs), 0) == row
        on_column = lax.broadcasted_iota(jnp.int32, (lon, n_obs), 0) == column
        wy = w * y
        parts = []
        for full in (w, wy):
            high = full.astype(jnp.bfloat16).astype(F32)
            for part in (high, full - high):
                parts.append(jnp.where(on_row, part, 0.0).astype(jnp.bfloat16))
        left = jnp.concatenate(parts, axis=0)
        right = jnp.where(on_column, 1.0, 0.0).astype(jnp.bfloat16)
        out = lax.dot_general(
            left, right, (((1,), (1,)), ((), ())), preferred_element_type=F32
        )
        return split(out[0:64] + out[64:128]), split(out[128:192] + out[192:256])

    def own_slot(s, carry):
        w, v = tables(cells[s], values[s], weights[s])
        WF[0, :, pl.ds(s, 64, stride=8), :] = w
        VF[0, :, pl.ds(s, 64, stride=8), :] = v
        return carry

    def kept_slot(s, carry):
        w, v = tables(cells[s + 4], values[s + 4], weights[s + 4])
        WF[0, :, pl.ds(s + 4, 64, stride=8), :] = w
        VF[0, :, pl.ds(s + 4, 64, stride=8), :] = v
        WF[1, :, pl.ds(s, 64, stride=8), :] = w
        VF[1, :, pl.ds(s, 64, stride=8), :] = v
        return carry

    def late_slot(s, carry):
        last = tm == n_tm - 1
        w, v = tables(
            jnp.where(last, f_cells[s], OC[s]),
            jnp.where(last, f_values[s], OV[s]),
            jnp.where(last, f_weights[s], OW[s]),
        )
        WF[1, :, pl.ds(s + 4, 64, stride=8), :] = w
        VF[1, :, pl.ds(s + 4, 64, stride=8), :] = v
        return carry

    lax.fori_loop(0, 4, own_slot, 0)
    lax.fori_loop(0, 4, kept_slot, 0)

    finish(moves)
    take_rows(0)

    @pl.when(lat > 0)
    def _():
        LF[:, pl.ds(0, 24), :] = HL[0]

    @pl.when(lat < n_lat - 1)
    def _():
        LF[:, pl.ds(536, 24), :] = HL[1]

    lane = lax.broadcasted_iota(jnp.int32, (1, 1, half_lon), 2)

    def other(x):
        return jnp.stack([x[1], x[0]])

    def from_east(x):
        turned = pltpu.roll(x, half_lon - 1, 2)
        return jnp.where(lane == half_lon - 1, other(turned), turned)

    def from_west(x):
        turned = pltpu.roll(x, 1, 2)
        return jnp.where(lane == 0, other(turned), turned)

    d, u, v = ND[0], 0.5 * ND[1], 0.5 * ND[2]
    row = lax.broadcasted_iota(jnp.int32, (2, 80, half_lon), 1) - 8 + lat * 64
    on_grid = jnp.logical_and(row >= 0, row < n_lat * 64)
    centre, north, south, east, west = 1.0 - 4.0 * d, d - v, d + v, d - u, d + u
    NF[0] = centre
    NF[1] = north
    NF[2] = south
    NF[3] = east
    NF[4] = west
    NB[0] = centre
    NB[1] = jnp.where(on_grid, pltpu.roll(south, 79, 1), 0.0)
    NB[2] = jnp.where(on_grid, pltpu.roll(north, 1, 1), 0.0)
    NB[3] = from_east(west)
    NB[4] = from_west(east)

    def spread(s, carry):
        for k in range(5):
            CF[k, :, pl.ds(s, 80, stride=8), :] = NF[k]
            CB[k, :, pl.ds(s, 80, stride=8), :] = NB[k]
        return carry

    lax.fori_loop(0, 8, spread, 0)

    def mix(c, mid, up, down):
        return (
            c[0] * mid
            + c[1] * up
            + c[2] * down
            + c[3] * from_east(mid)
            + c[4] * from_west(mid)
        )

    def rows_of(ref, coef, first, r, size):
        f = ref[:, pl.ds(r * 8, (size + 2) * 8), :]
        c = [coef[k, :, pl.ds((first + r) * 8, size * 8), :] for k in range(5)]
        return mix(c, f[:, 8 : 8 + size * 8], f[:, 16:], f[:, : size * 8])

    def over_rows(count, size, body):
        def step(i, carry):
            body(pl.multiple_of(i * size, size), size)
            return carry

        lax.fori_loop(0, count // size, step, 0)
        if count % size:
            body(count - count % size, count % size)

    def sweep3(src, coef, first, dst, count):
        def body(r, size):
            dst[:, pl.ds(r * 8, size * 8), :] = rows_of(src, coef, first, r, size)

        over_rows(count, 8, body)

    slot = lax.broadcasted_iota(jnp.int32, (1, 1, 8, half_lon), 2)

    def cube(x):
        return x.reshape(2, x.shape[1] // 8, 8, half_lon)

    def flat(x):
        return x.reshape(2, x.shape[1] * 8, half_lon)

    def lone(field, coef, at, stride, levels):
        for level in range(levels):
            c = [
                [coef[k, :, pl.ds(at + level + 1 + q, 8, stride=stride), :] for k in range(5)]
                for q in range(len(field) - 2)
            ]
            field = [
                mix(c[q], field[q + 1], field[q + 2], field[q]) for q in range(len(field) - 2)
            ]
        return field

    def forward_part(r, window):
        sweep3(XF, CF, 3, T1, 74)
        sweep3(T1, CF, 4, T2, 72)

        def last(q, size):
            y = rows_of(T2, CF, 5, q, size)
            T1[:, pl.ds(q * 8, size * 8), :] = y
            x = XF[:, pl.ds((q + 3) * 8, size * 8), :]
            jump = jnp.where(slot > 0, cube(x) - pltpu.roll(cube(y), 1, 2), 0.0)
            LF[:, pl.ds(q * 8, size * 8), :] += flat(jump)

        over_rows(70, 8, last)
        before = [E[r, :, pl.ds(2 + q, 8, stride=9), :] for q in range(15)]
        before = lone(before, NF, 2, 9, 3)
        share = jnp.where(tm == 0, 0.0, 1.0) if window == 0 else None
        after = jnp.where(tm == n_tm - 1, 0.0, 1.0)
        for q in range(9):
            jump = XF[:, pl.ds((q + 3) * 8, 8, stride=72), :] - before[q]
            if share is not None:
                jump = share * jump
            LF[:, pl.ds(q * 8, 8, stride=72), :] += jump
            jump = NX[r, :, pl.ds(5 + q, 8, stride=9), :]
            jump = jump - T1[:, pl.ds(q * 8 + 7, 8, stride=72), :]
            NL[window, :, pl.ds(5 + q, 8, stride=9), :] += after * jump

    def backward_part(window):
        sweep3(LF, CB, 6, T1, 68)
        sweep3(T1, CB, 7, T2, 66)

        def last(q, size):
            g = cube(rows_of(T2, CB, 8, q, size))
            g = flat(jnp.where(slot < 7, pltpu.roll(g, 7, 2), 0.0))
            x = XF[:, pl.ds((q + 6) * 8, size * 8), :]
            p = LF[:, pl.ds((q + 3) * 8, size * 8), :]
            w = WF[window, :, pl.ds(q * 8, size * 8), :]
            y = VF[window, :, pl.ds(q * 8, size * 8), :]
            XF[:, pl.ds((q + 6) * 8, size * 8), :] = x - STEP * (w * x - y + p - g)

        over_rows(64, 8, last)
        after = [NL[window, :, pl.ds(5 + q, 8, stride=8), :] for q in range(14)]
        after = lone(after, NB, 5, 8, 3)
        for q in range(8):
            XF[:, pl.ds((q + 6) * 8 + 7, 8, stride=64), :] += STEP * after[q]

    forward_part(0, 0)
    backward_part(0)
    edges(1)
    moves = send_rows(1) + send_before(1) + send_after(1)
    finish(obs_moves)
    lax.fori_loop(0, 4, late_slot, 0)
    finish(moves)
    take_rows(1)
    forward_part(1, 0)

    low = slot < 4

    def pairs(v):
        return v.reshape(2, v.shape[1] // 16, 2, 8, half_lon)

    def pack(src, first, dst, count, size):
        def body(i, carry):
            v = pairs(src[:, pl.ds((first + i * size * 2) * 8, size * 16), :])
            v = jnp.where(low, v[:, :, 0], pltpu.roll(v[:, :, 1], 4, 2))
            dst[:, pl.ds(i * size * 8, size * 8), :] = flat(v)
            return carry

        lax.fori_loop(0, count // size, body, 0)

    def unpack(src, dst, count, size, fill):
        def body(i, carry):
            v = pairs(dst[:, pl.ds(i * size * 16, size * 16), :])
            p = cube(src[:, pl.ds(i * size * 8, size * 8), :])
            out = []
            for half, q in ((v[:, :, 0], pltpu.roll(p, 4, 2)), (v[:, :, 1], p)):
                q = jnp.where(tm == n_tm - 1, fill(half), q)
                out.append(jnp.where(low, pltpu.roll(half, 4, 2), q))
            out = jnp.stack(out, axis=2)
            dst[:, pl.ds(i * size * 16, size * 16), :] = out.reshape(2, size * 16, half_lon)
            return carry

        lax.fori_loop(0, count // size, body, 0)

    pack(LF, 0, PKL, 35, 5)
    SL4[:, pl.ds(5, 70), :] = LF[:, pl.ds(4, 70, stride=8), :]
    early = [Move(PKL, RKL, -1, 0), Move(SL4, NL.at[1], -1, 0)]
    backward_part(0)
    pack(XF, 6, PKX, 32, 4)
    S0[2] = XF[:, pl.ds(52, 64, stride=8), :]
    moves = send_rows(2) + [
        Move(PKX, RKX.at[:, pl.ds(24, 256)], -1, 0),
        Move(PKX.at[:, pl.ds(0, 24)], RKX.at[:, pl.ds(280, 24)], -1, -1),
        Move(PKX.at[:, pl.ds(232, 24)], RKX.at[:, pl.ds(0, 24)], -1, 1),
    ]
    moves += send_after(2)
    finish(early)
    unpack(RKL, LF, 35, 5, jnp.zeros_like)
    finish(moves)
    take_rows(2)
    E[2, :, pl.ds(2, 76), :] = XF[:, pl.ds(3, 76, stride=8), :]
    unpack(RKX, XF, 38, 2, lambda half: jnp.broadcast_to(half[:, :, 7:8], half.shape))

    forward_part(2, 1)
    backward_part(1)
    edges(3)
    moves = send_rows(3) + send_before(3) + send_after(3)

    @pl.when(tm == 0)
    def _():
        E[3] = E[2]

    finish(moves)
    take_rows(3)
    forward_part(3, 1)
    backward_part(1)
    for s in range(8):
        x_out[s] = join(XF[:, pl.ds(48 + s, 64, stride=8), :])
        l_out[s] = join(LF[:, pl.ds(24 + s, 64, stride=8), :])
    assert made[0] == n_transfers


def body(n_tm, n_lat, *arrays):
    states = arrays[0]
    slots, rows, lon = states.shape
    n_obs = arrays[5].shape[-1]
    n_transfers = 44

    def vmem(*shape, kind=F32):
        return pltpu.VMEM(shape, kind)

    shape = jax.ShapeDtypeStruct((slots, rows, lon), F32)
    return pl.pallas_call(
        functools.partial(weave, n_tm, n_lat, n_transfers),
        out_shape=(shape, shape),
        in_specs=[pl.BlockSpec(memory_space=pltpu.VMEM)] * len(arrays),
        out_specs=(pl.BlockSpec(memory_space=pltpu.VMEM),) * 2,
        scratch_shapes=[
            vmem(2, 640, lon // 2),
            vmem(2, 576, lon // 2),
            vmem(2, 592, lon // 2),
            vmem(2, 576, lon // 2),
            vmem(5, 2, 640, lon // 2),
            vmem(5, 2, 640, lon // 2),
            vmem(3, 2, 80, lon // 2),
            vmem(5, 2, 80, lon // 2),
            vmem(5, 2, 80, lon // 2),
            vmem(2, 2, 512, lon // 2),
            vmem(2, 2, 512, lon // 2),
            vmem(4, 2, 2, 48, lon // 2),
            vmem(2, 2, 24, lon // 2),
            vmem(4, 2, 80, lon // 2),
            vmem(4, 2, 80, lon // 2),
            vmem(2, 2, 80, lon // 2),
            vmem(4, 2, 64, lon // 2),
            vmem(4, 2, 64, lon // 2),
            vmem(2, 64, lon // 2),
            vmem(2, 256, lon // 2),
            vmem(2, 280, lon // 2),
            vmem(2, 80, lon // 2),
            vmem(2, 304, lon // 2),
            vmem(2, 280, lon // 2),
            vmem(4, 1, n_obs, kind=jnp.int32),
            vmem(4, 1, n_obs),
            vmem(4, 1, n_obs),
            pltpu.SemaphoreType.DMA((n_transfers,)),
            pltpu.SemaphoreType.DMA((n_transfers,)),
        ],
        compiler_params=pltpu.CompilerParams(
            collective_id=0, has_side_effects=True, vmem_limit_bytes=48 * 1024 * 1024
        ),
    )(*arrays)


def solution(mesh):
    field = P("tm", "lat", None)
    plane = P("lat", None)
    fresh = P(None, "lat", None)
    in_specs = (field, field, plane, plane, plane, field, field, field, fresh, fresh, fresh)
    return jax.shard_map(
        functools.partial(body, mesh.shape["tm"], mesh.shape["lat"]),
        mesh=mesh,
        in_specs=in_specs,
        out_specs=(field, field),
        check_vma=False,
    )
```

```python
import functools

import jax
import jax.numpy as jnp
from jax import lax
from jax.experimental import pallas as pl
from jax.experimental.pallas import tpu as pltpu
from jax.sharding import PartitionSpec as P

MESH = pl.DeviceIdType.MESH
STEP = 0.15
F32 = jnp.float32


def weave(n_tm, n_lat, n_transfers, *refs):
    (
        states_hbm,
        mults_hbm,
        diff_hbm,
        zonal_hbm,
        merid_hbm,
        cells_hbm,
        values_hbm,
        weights_hbm,
        f_cells_hbm,
        f_values_hbm,
        f_weights_hbm,
        x_out,
        l_out,
        XF,
        LF,
        T1,
        T2,
        Y,
        U1,
        U2,
        CF,
        CB,
        ND,
        NF,
        NB,
        WF,
        VF,
        HX,
        HL,
        E,
        NX,
        NL,
        S7,
        S0,
        SL0,
        PKX,
        PKL,
        SL4,
        RKX,
        RKL,
        states,
        mults,
        speeds,
        cells,
        values,
        weights,
        ssem,
        rsem,
        lsem,
    ) = refs
    lon = 2 * XF.shape[-1]
    half_lon = lon // 2
    tm = lax.axis_index("tm")
    lat = lax.axis_index("lat")
    made = [0]

    def inside(dt, dl):
        ok = True
        if dt > 0:
            ok = tm < n_tm - 1
        elif dt < 0:
            ok = tm > 0
        if dl > 0:
            ok = jnp.logical_and(ok, lat < n_lat - 1)
        elif dl < 0:
            ok = jnp.logical_and(ok, lat > 0)
        return ok

    class Move:
        def __init__(self, src, dst, dt, dl):
            i = made[0]
            made[0] += 1
            assert i < n_transfers
            self.to, self.by = inside(dt, dl), inside(-dt, -dl)
            self.copy = pltpu.make_async_remote_copy(
                src_ref=src,
                dst_ref=dst,
                send_sem=ssem.at[i],
                recv_sem=rsem.at[i],
                device_id=(tm + dt, lat + dl),
                device_id_type=MESH,
            )
            pl.when(self.to)(self.copy.start)

        def sent(self):
            pl.when(self.to)(self.copy.wait_send)
            self.to = None

        def finish(self):
            if self.to is not None:
                self.sent()
            pl.when(self.by)(self.copy.wait_recv)

    fetched = [
        pltpu.make_async_copy(src, dst, lsem.at[i])
        for i, (src, dst) in enumerate(
            (
                (states_hbm, states),
                (mults_hbm, mults),
                (diff_hbm, speeds.at[0]),
                (zonal_hbm, speeds.at[1]),
                (merid_hbm, speeds.at[2]),
                (cells_hbm, cells.at[pl.ds(0, 8)]),
                (values_hbm, values.at[pl.ds(0, 8)]),
                (weights_hbm, weights.at[pl.ds(0, 8)]),
            )
        )
    ]
    for copy in fetched:
        copy.start()
    fresh = [
        pltpu.make_async_copy(src, dst.at[pl.ds(8, 4)], lsem.at[8 + i])
        for i, (src, dst) in enumerate(
            ((f_cells_hbm, cells), (f_values_hbm, values), (f_weights_hbm, weights))
        )
    ]

    @pl.when(tm == n_tm - 1)
    def _():
        for copy in fresh:
            copy.start()

    barrier = pltpu.get_barrier_semaphore()
    greeted = 0
    for dt in (-1, 0, 1):
        for dl in (-1, 0, 1):
            if dt == 0 and dl == 0:
                continue
            ok = inside(dt, dl)

            @pl.when(ok)
            def _():
                pl.semaphore_signal(
                    barrier, inc=1, device_id=(tm + dt, lat + dl), device_id_type=MESH
                )

            greeted = greeted + ok.astype(jnp.int32)

    whole = slice(None)

    def blank(ref, *at):
        ref[at] = jnp.zeros(ref.at[at].shape, ref.dtype)

    @pl.when(lat == 0)
    def _():
        for r in range(4):
            blank(E, r, whole, slice(0, 8))
            blank(NX, r, whole, slice(0, 8))
        for k in range(3):
            blank(ND, k, whole, slice(0, 8))
        blank(NL, 0, whole, slice(0, 8))
        blank(XF, whole, slice(0, 48))
        blank(LF, whole, slice(0, 24))
        blank(RKX, whole, slice(0, 24))

    @pl.when(lat == n_lat - 1)
    def _():
        for r in range(4):
            blank(E, r, whole, slice(72, 80))
            blank(NX, r, whole, slice(72, 80))
        for k in range(3):
            blank(ND, k, whole, slice(72, 80))
        blank(NL, 0, whole, slice(72, 80))
        blank(XF, whole, slice(560, 608))
        blank(LF, whole, slice(536, 560))
        blank(RKX, whole, slice(280, 304))

    @pl.when(tm == 0)
    def _():
        blank(E, 0)
        blank(E, 1)

    @pl.when(tm == n_tm - 1)
    def _():
        for r in range(4):
            blank(NX, r)
        blank(NL, 0)
        blank(NL, 1)

    blank(XF, whole, slice(608, 640))
    blank(E, 2, whole, slice(72, 80))
    blank(LF, whole, slice(560, 576))

    def split(x):
        return jnp.stack([x[:, :half_lon], x[:, half_lon:]])

    def join(x):
        return jnp.concatenate([x[0], x[1]], axis=1)

    for copy in fetched[:5]:
        copy.wait()
    for s in range(8):
        XF[:, pl.ds(48 + s, 64, stride=8), :] = split(states[s])
        LF[:, pl.ds(24 + s, 64, stride=8), :] = split(mults[s])
    S7[0] = split(states[7])
    S0[0] = split(states[0])
    SL0[...] = split(mults[0])
    for k in range(3):
        ND[k, :, pl.ds(8, 64), :] = split(speeds[k])

    pl.semaphore_wait(barrier, greeted)

    def send_corners(r, before=True):
        moves = []
        if before:
            moves += [
                Move(S7.at[r, :, pl.ds(0, 8)], E.at[r, :, pl.ds(72, 8)], 1, -1),
                Move(S7.at[r, :, pl.ds(56, 8)], E.at[r, :, pl.ds(0, 8)], 1, 1),
            ]
        return moves + [
            Move(S0.at[r, :, pl.ds(0, 8)], NX.at[r, :, pl.ds(72, 8)], -1, -1),
            Move(S0.at[r, :, pl.ds(56, 8)], NX.at[r, :, pl.ds(0, 8)], -1, 1),
        ]

    def send_slots(r, before=True):
        moves = [Move(S7.at[r], E.at[r, :, pl.ds(8, 64)], 1, 0)] if before else []
        return moves + [Move(S0.at[r], NX.at[r, :, pl.ds(8, 64)], -1, 0)]

    def send_rows(r):
        return [
            Move(XF.at[:, pl.ds(48, 48)], HX.at[r, 1], 0, -1),
            Move(XF.at[:, pl.ds(512, 48)], HX.at[r, 0], 0, 1),
        ]

    def finish(moves):
        for move in moves:
            move.finish()

    def take_rows(r):
        @pl.when(lat > 0)
        def _():
            XF[:, pl.ds(0, 48), :] = HX[r, 0]

        @pl.when(lat < n_lat - 1)
        def _():
            XF[:, pl.ds(560, 48), :] = HX[r, 1]

    def edges(r):
        S7[r] = XF[:, pl.ds(55, 64, stride=8), :]
        S0[r] = XF[:, pl.ds(48, 64, stride=8), :]

    slot_moves = send_corners(0) + [
        Move(SL0.at[:, pl.ds(0, 8)], NL.at[0, :, pl.ds(72, 8)], -1, -1),
        Move(SL0.at[:, pl.ds(56, 8)], NL.at[0, :, pl.ds(0, 8)], -1, 1),
    ]
    row_moves = send_rows(0)
    row_moves += [
        Move(LF.at[:, pl.ds(24, 24)], HL.at[1], 0, -1),
        Move(LF.at[:, pl.ds(512, 24)], HL.at[0], 0, 1),
        Move(ND.at[:, :, pl.ds(8, 8)], ND.at[:, :, pl.ds(72, 8)], 0, -1),
        Move(ND.at[:, :, pl.ds(64, 8)], ND.at[:, :, pl.ds(0, 8)], 0, 1),
    ]
    slot_moves += send_slots(0) + [Move(SL0, NL.at[0, :, pl.ds(8, 64)], -1, 0)]
    for copy in fetched[5:]:
        copy.wait()
    obs_moves = [
        Move(cells.at[pl.ds(0, 4)], cells.at[pl.ds(8, 4)], -1, 0),
        Move(values.at[pl.ds(0, 4)], values.at[pl.ds(8, 4)], -1, 0),
        Move(weights.at[pl.ds(0, 4)], weights.at[pl.ds(8, 4)], -1, 0),
    ]

    n_obs = cells.shape[-1]

    def tables(c, y, w):
        row = lax.shift_right_logical(c, 8)
        column = lax.bitwise_and(c, 255)
        on_row = lax.broadcasted_iota(jnp.int32, (64, n_obs), 0) == row
        on_column = lax.broadcasted_iota(jnp.int32, (lon, n_obs), 0) == column
        wy = w * y
        parts = []
        for full in (w, wy):
            high = full.astype(jnp.bfloat16).astype(F32)
            for part in (high, full - high):
                parts.append(jnp.where(on_row, part, 0.0).astype(jnp.bfloat16))
        left = jnp.concatenate(parts, axis=0)
        right = jnp.where(on_column, 1.0, 0.0).astype(jnp.bfloat16)
        out = lax.dot_general(
            left, right, (((1,), (1,)), ((), ())), preferred_element_type=F32
        )
        return split(out[0:64] + out[64:128]), split(out[128:192] + out[192:256])

    def own_slot(s, carry):
        w, v = tables(cells[s], values[s], weights[s])
        WF[0, :, pl.ds(s, 64, stride=8), :] = w
        VF[0, :, pl.ds(s, 64, stride=8), :] = v
        return carry

    def kept_slot(s, carry):
        w, v = tables(cells[s + 4], values[s + 4], weights[s + 4])
        WF[0, :, pl.ds(s + 4, 64, stride=8), :] = w
        VF[0, :, pl.ds(s + 4, 64, stride=8), :] = v
        WF[1, :, pl.ds(s, 64, stride=8), :] = w
        VF[1, :, pl.ds(s, 64, stride=8), :] = v
        return carry

    def late_slot(s, carry):
        w, v = tables(cells[s + 8], values[s + 8], weights[s + 8])
        WF[1, :, pl.ds(s + 4, 64, stride=8), :] = w
        VF[1, :, pl.ds(s + 4, 64, stride=8), :] = v
        return carry

    lane = lax.broadcasted_iota(jnp.int32, (1, 1, half_lon), 2)

    def other(x):
        return jnp.stack([x[1], x[0]])

    def from_east(x):
        turned = pltpu.roll(x, half_lon - 1, 2)
        return jnp.where(lane == half_lon - 1, other(turned), turned)

    def from_west(x):
        turned = pltpu.roll(x, 1, 2)
        return jnp.where(lane == 0, other(turned), turned)

    def combine(first, count, kept):
        rows = pl.ds(first, count)
        d, u, v = ND[0, :, rows, :], 0.5 * ND[1, :, rows, :], 0.5 * ND[2, :, rows, :]
        row = lax.broadcasted_iota(jnp.int32, (2, count, half_lon), 1) + (first - 8) + lat * 64
        on_grid = jnp.logical_and(row >= 0, row < n_lat * 64)
        centre, north, south, east, west = 1.0 - 4.0 * d, d - v, d + v, d - u, d + u
        here = pl.ds(first + kept.start, kept.stop - kept.start)
        for k, value in enumerate((centre, north, south, east, west)):
            NF[k, :, here, :] = value[:, kept]
        adjoint = (
            centre,
            jnp.where(on_grid, pltpu.roll(south, count - 1, 1), 0.0),
            jnp.where(on_grid, pltpu.roll(north, 1, 1), 0.0),
            from_east(west),
            from_west(east),
        )
        for k, value in enumerate(adjoint):
            NB[k, :, here, :] = value[:, kept]

    def spread(first, count):
        def body(s, carry):
            for k in range(5):
                at = pl.ds(first * 8 + s, count, stride=8)
                CF[k, :, at, :] = NF[k, :, pl.ds(first, count), :]
                CB[k, :, at, :] = NB[k, :, pl.ds(first, count), :]
            return carry

        lax.fori_loop(0, 8, body, 0)

    def mix(c, mid, up, down):
        return (
            c[0] * mid
            + c[1] * up
            + c[2] * down
            + c[3] * from_east(mid)
            + c[4] * from_west(mid)
        )

    def tile(row, off):
        return pl.ds((row + off) * 8, 8)

    def one(src, off, coef, row):
        f = [src[:, tile(row + j, off), :] for j in (-1, 0, 1)]
        c = [coef[k, :, tile(row, 8), :] for k in range(5)]
        return mix(c, f[1], f[2], f[0])

    def over(rows, work):
        calc, store = work
        done = [calc(row) for row in rows]
        for row, value in zip(rows, done):
            store(row, value)

    def between(low, high, work):
        size = (high - low) // 2

        def step(i, carry):
            over([low + i * size + q for q in range(size)], work)
            return carry

        lax.fori_loop(0, 2, step, 0)

    def substep(src, off, coef, dst, dst_off):
        def store(row, value):
            dst[:, tile(row, dst_off), :] = value

        return (lambda row: one(src, off, coef, row)), store

    slot = lax.broadcasted_iota(jnp.int32, (1, 8, half_lon), 1)

    def cube(x):
        return x.reshape(2, x.shape[1] // 8, 8, half_lon)

    def flat(x):
        return x.reshape(2, x.shape[1] * 8, half_lon)

    def lone(field, coef, at, stride, levels):
        for level in range(levels):
            c = [
                [coef[k, :, pl.ds(at + level + 1 + q, 8, stride=stride), :] for k in range(5)]
                for q in range(len(field) - 2)
            ]
            field = [
                mix(c[q], field[q + 1], field[q + 2], field[q]) for q in range(len(field) - 2)
            ]
        return field

    def works(window):
        share = jnp.where(tm == 0, 0.0, 1.0) if window == 0 else 1.0

        def calc_jump(row):
            y = one(T2, 4, CF, row)
            x = XF[:, tile(row, 6), :]
            jump = jnp.where(slot > 0, x - pltpu.roll(y, 1, 1), share * x)
            return y, LF[:, tile(row, 3), :] + jump

        def store_jump(row, value):
            Y[:, tile(row, 3), :] = value[0]
            LF[:, tile(row, 3), :] = value[1]

        def calc_state(row):
            g = one(U2, 1, CB, row)
            g = jnp.where(slot < 7, pltpu.roll(g, 7, 1), 0.0)
            x = XF[:, tile(row, 6), :]
            p = LF[:, tile(row, 3), :]
            w = WF[window, :, tile(row, 0), :]
            y = VF[window, :, tile(row, 0), :]
            return x - STEP * (w * x - y + p - g)

        def store_state(row, value):
            XF[:, tile(row, 6), :] = value

        return (
            substep(XF, 6, CF, T1, 5),
            substep(T1, 5, CF, T2, 4),
            (calc_jump, store_jump),
            substep(LF, 3, CB, U1, 2),
            substep(U1, 2, CB, U2, 1),
            (calc_state, store_state),
        )

    def interior(window):
        for i, work in enumerate(works(window)):
            between(1 + i, 63 - i, work)

    def ends(window):
        for i, work in enumerate(works(window)):
            over([row for row in range(i - 5, i + 1)] + [row for row in range(63 - i, 69 - i)], work)

    def slots_beside(r, window):
        before = [E[r, :, pl.ds(2 + q, 8, stride=9), :] for q in range(15)]
        before = lone(before, NF, 2, 9, 3)
        after_on = jnp.where(tm == n_tm - 1, 0.0, 1.0)
        for q in range(9):
            jump = NX[r, :, pl.ds(5 + q, 8, stride=9), :]
            jump = jump - Y[:, pl.ds(q * 8 + 7, 8, stride=72), :]
            NL[window, :, pl.ds(5 + q, 8, stride=9), :] += after_on * jump
        after = [NL[window, :, pl.ds(5 + q, 8, stride=8), :] for q in range(14)]
        after = lone(after, NB, 5, 8, 3)
        for q in range(9):
            first = before[q]
            if window == 0:
                first = jnp.where(tm == 0, 0.0, 1.0) * first
            LF[:, pl.ds(q * 8, 8, stride=72), :] -= first
            XF[:, pl.ds((q + 3) * 8, 8, stride=72), :] += STEP * first
        for q in range(8):
            XF[:, pl.ds((q + 6) * 8 + 7, 8, stride=64), :] += STEP * after[q]

    combine(8, 64, slice(0, 64))
    spread(8, 64)
    lax.fori_loop(0, 4, own_slot, 0)
    lax.fori_loop(0, 4, kept_slot, 0)
    interior(0)
    finish(row_moves)
    take_rows(0)

    @pl.when(lat > 0)
    def _():
        LF[:, pl.ds(0, 24), :] = HL[0]

    @pl.when(lat < n_lat - 1)
    def _():
        LF[:, pl.ds(536, 24), :] = HL[1]

    combine(0, 24, slice(0, 16))
    combine(56, 24, slice(8, 24))
    spread(0, 16)
    spread(64, 16)
    ends(0)
    finish(slot_moves)
    slots_beside(0, 0)
    edges(1)
    slot_moves = send_corners(1)
    row_moves = send_rows(1)
    slot_moves += send_slots(1)
    interior(0)
    finish(obs_moves)

    @pl.when(tm == n_tm - 1)
    def _():
        for copy in fresh:
            copy.wait()

    lax.fori_loop(0, 4, late_slot, 0)
    finish(row_moves)
    take_rows(1)
    ends(0)
    finish(slot_moves)
    slots_beside(1, 0)

    low = lax.broadcasted_iota(jnp.int32, (1, 1, 8, half_lon), 2) < 4

    def pairs(v):
        return v.reshape(2, v.shape[1] // 16, 2, 8, half_lon)

    def pack(src, first, dst, count, size):
        def body(i, carry):
            v = pairs(src[:, pl.ds((first + i * size * 2) * 8, size * 16), :])
            v = jnp.where(low, v[:, :, 0], pltpu.roll(v[:, :, 1], 4, 2))
            dst[:, pl.ds(i * size * 8, size * 8), :] = flat(v)
            return carry

        lax.fori_loop(0, count // size, body, 0)

    def unpack(src, dst, first, count, size, fill):
        def body(i, carry):
            at = first + i * size
            v = pairs(dst[:, pl.ds(at * 16, size * 16), :])
            p = cube(src[:, pl.ds(at * 8, size * 8), :])
            out = []
            for half, q in ((v[:, :, 0], pltpu.roll(p, 4, 2)), (v[:, :, 1], p)):
                q = jnp.where(tm == n_tm - 1, fill(half), q)
                out.append(jnp.where(low, pltpu.roll(half, 4, 2), q))
            out = jnp.stack(out, axis=2)
            dst[:, pl.ds(at * 16, size * 16), :] = out.reshape(2, size * 16, half_lon)
            return carry

        lax.fori_loop(0, count // size, body, 0)

    pack(LF, 0, PKL, 35, 5)
    SL4[:, pl.ds(5, 70), :] = LF[:, pl.ds(4, 70, stride=8), :]
    early = [Move(PKL, RKL, -1, 0), Move(SL4, NL.at[1], -1, 0)]
    pack(XF, 6, PKX, 32, 4)
    S0[2] = XF[:, pl.ds(52, 64, stride=8), :]
    slot_moves = send_corners(2, before=False)
    corner_moves = [
        Move(PKX.at[:, pl.ds(0, 24)], RKX.at[:, pl.ds(280, 24)], -1, -1),
        Move(PKX.at[:, pl.ds(232, 24)], RKX.at[:, pl.ds(0, 24)], -1, 1),
    ]
    row_moves = send_rows(2)
    slab_moves = [Move(PKX, RKX.at[:, pl.ds(24, 256)], -1, 0)]
    slot_moves += send_slots(2, before=False)
    E[2, :, pl.ds(8, 64), :] = XF[:, pl.ds(51, 64, stride=8), :]

    def repeat(half):
        return jnp.broadcast_to(half[:, :, 7:8], half.shape)

    finish(early)
    unpack(RKL, LF, 0, 35, 5, jnp.zeros_like)
    finish(slab_moves)
    for move in row_moves:
        move.sent()
    unpack(RKX, XF, 3, 32, 8, repeat)

    interior(1)
    finish(row_moves)
    take_rows(2)
    E[2, :, pl.ds(2, 6), :] = XF[:, pl.ds(3, 6, stride=8), :]
    E[2, :, pl.ds(72, 6), :] = XF[:, pl.ds(563, 6, stride=8), :]
    finish(corner_moves)
    unpack(RKX, XF, 0, 3, 3, repeat)
    unpack(RKX, XF, 35, 3, 3, repeat)
    ends(1)
    finish(slot_moves)
    slots_beside(2, 1)
    edges(3)
    slot_moves = send_corners(3)
    row_moves = send_rows(3)
    slot_moves += send_slots(3)

    @pl.when(tm == 0)
    def _():
        E[3] = E[2]

    interior(1)
    finish(row_moves)
    take_rows(3)
    ends(1)
    finish(slot_moves)
    slots_beside(3, 1)
    results = [
        pltpu.make_async_copy(XF.at[:, pl.ds(48, 512)], x_out, lsem.at[0]),
        pltpu.make_async_copy(LF.at[:, pl.ds(24, 512)], l_out, lsem.at[1]),
    ]
    for copy in results:
        copy.start()
    for copy in results:
        copy.wait()
    assert made[0] == n_transfers


def unweave(x_hbm, l_hbm, x_out, l_out, x_ref, l_ref, sems):
    copies = [
        pltpu.make_async_copy(src, dst, sems.at[i])
        for i, (src, dst) in enumerate(((x_hbm, x_ref), (l_hbm, l_ref)))
    ]
    for copy in copies:
        copy.start()
    for copy, ref, out in zip(copies, (x_ref, l_ref), (x_out, l_out)):
        copy.wait()
        for s in range(8):
            x = ref[:, pl.ds(s, 64, stride=8), :]
            out[s] = jnp.concatenate([x[0], x[1]], axis=1)


def body(n_tm, n_lat, *arrays):
    states = arrays[0]
    slots, rows, lon = states.shape
    n_obs = arrays[5].shape[-1]
    n_transfers = 44

    def vmem(*shape, kind=F32):
        return pltpu.VMEM(shape, kind)

    woven = jax.ShapeDtypeStruct((2, slots * rows, lon // 2), F32)
    shape = jax.ShapeDtypeStruct((slots, rows, lon), F32)
    fields = pl.pallas_call(
        functools.partial(weave, n_tm, n_lat, n_transfers),
        out_shape=(woven, woven),
        in_specs=[pl.BlockSpec(memory_space=pltpu.HBM)] * len(arrays),
        out_specs=(pl.BlockSpec(memory_space=pltpu.HBM),) * 2,
        scratch_shapes=[
            vmem(2, 640, lon // 2),
            vmem(2, 576, lon // 2),
            vmem(2, 592, lon // 2),
            vmem(2, 576, lon // 2),
            vmem(2, 576, lon // 2),
            vmem(2, 544, lon // 2),
            vmem(2, 528, lon // 2),
            vmem(5, 2, 640, lon // 2),
            vmem(5, 2, 640, lon // 2),
            vmem(3, 2, 80, lon // 2),
            vmem(5, 2, 80, lon // 2),
            vmem(5, 2, 80, lon // 2),
            vmem(2, 2, 512, lon // 2),
            vmem(2, 2, 512, lon // 2),
            vmem(4, 2, 2, 48, lon // 2),
            vmem(2, 2, 24, lon // 2),
            vmem(4, 2, 80, lon // 2),
            vmem(4, 2, 80, lon // 2),
            vmem(2, 2, 80, lon // 2),
            vmem(4, 2, 64, lon // 2),
            vmem(4, 2, 64, lon // 2),
            vmem(2, 64, lon // 2),
            vmem(2, 256, lon // 2),
            vmem(2, 280, lon // 2),
            vmem(2, 80, lon // 2),
            vmem(2, 304, lon // 2),
            vmem(2, 280, lon // 2),
            vmem(slots, rows, lon),
            vmem(slots, rows, lon),
            vmem(3, rows, lon),
            vmem(12, 1, n_obs, kind=jnp.int32),
            vmem(12, 1, n_obs),
            vmem(12, 1, n_obs),
            pltpu.SemaphoreType.DMA((n_transfers,)),
            pltpu.SemaphoreType.DMA((n_transfers,)),
            pltpu.SemaphoreType.DMA((11,)),
        ],
        compiler_params=pltpu.CompilerParams(
            collective_id=0, has_side_effects=True, vmem_limit_bytes=64 * 1024 * 1024 - 65536
        ),
    )(*arrays)
    return pl.pallas_call(
        unweave,
        out_shape=(shape, shape),
        in_specs=[pl.BlockSpec(memory_space=pltpu.HBM)] * 2,
        out_specs=(pl.BlockSpec(memory_space=pltpu.VMEM),) * 2,
        scratch_shapes=[
            vmem(2, 512, lon // 2),
            vmem(2, 512, lon // 2),
            pltpu.SemaphoreType.DMA((2,)),
        ],
        compiler_params=pltpu.CompilerParams(vmem_limit_bytes=64 * 1024 * 1024 - 65536),
    )(*fields)


def solution(mesh):
    field = P("tm", "lat", None)
    plane = P("lat", None)
    fresh = P(None, "lat", None)
    in_specs = (field, field, plane, plane, plane, field, field, field, fresh, fresh, fresh)
    return jax.shard_map(
        functools.partial(body, mesh.shape["tm"], mesh.shape["lat"]),
        mesh=mesh,
        in_specs=in_specs,
        out_specs=(field, field),
        check_vma=False,
    )
```

```python
import functools

import jax
import jax.numpy as jnp
from jax import lax
from jax.experimental import pallas as pl
from jax.experimental.pallas import tpu as pltpu
from jax.sharding import PartitionSpec as P

MESH = pl.DeviceIdType.MESH
STEP = 0.15
F32 = jnp.float32


def weave(n_tm, n_lat, n_transfers, *refs):
    (
        states_hbm,
        mults_hbm,
        diff_hbm,
        zonal_hbm,
        merid_hbm,
        cells_hbm,
        values_hbm,
        weights_hbm,
        f_cells_hbm,
        f_values_hbm,
        f_weights_hbm,
        x_out,
        l_out,
        XF,
        LF,
        T1,
        T2,
        Y,
        U1,
        U2,
        CF,
        CB,
        ND,
        NF,
        NB,
        WF,
        VF,
        HX,
        HL,
        E,
        NX,
        NL,
        S7,
        S0,
        SL0,
        PKX,
        PKL,
        SL4,
        RKX,
        RKL,
        SXZ,
        SLZ,
        RXZ,
        RLZ,
        states,
        mults,
        speeds,
        cells,
        values,
        weights,
        ssem,
        rsem,
        lsem,
    ) = refs
    lon = 2 * XF.shape[-1]
    half_lon = lon // 2
    tm = lax.axis_index("tm")
    lat = lax.axis_index("lat")
    made = [0]

    def inside(dt, dl):
        ok = True
        if dt > 0:
            ok = tm < n_tm - 1
        elif dt < 0:
            ok = tm > 0
        if dl > 0:
            ok = jnp.logical_and(ok, lat < n_lat - 1)
        elif dl < 0:
            ok = jnp.logical_and(ok, lat > 0)
        return ok

    class Move:
        def __init__(self, src, dst, dt, dl):
            i = made[0]
            made[0] += 1
            assert i < n_transfers
            self.to, self.by = inside(dt, dl), inside(-dt, -dl)
            self.copy = pltpu.make_async_remote_copy(
                src_ref=src,
                dst_ref=dst,
                send_sem=ssem.at[i],
                recv_sem=rsem.at[i],
                device_id=(tm + dt, lat + dl),
                device_id_type=MESH,
            )
            pl.when(self.to)(self.copy.start)

        def sent(self):
            pl.when(self.to)(self.copy.wait_send)
            self.to = None

        def finish(self):
            if self.to is not None:
                self.sent()
            pl.when(self.by)(self.copy.wait_recv)

    fetched = [
        pltpu.make_async_copy(src, dst, lsem.at[i])
        for i, (src, dst) in enumerate(
            (
                (states_hbm, states),
                (mults_hbm, mults),
                (diff_hbm, speeds.at[0]),
                (zonal_hbm, speeds.at[1]),
                (merid_hbm, speeds.at[2]),
                (cells_hbm, cells.at[pl.ds(0, 8)]),
                (values_hbm, values.at[pl.ds(0, 8)]),
                (weights_hbm, weights.at[pl.ds(0, 8)]),
            )
        )
    ]
    for copy in fetched:
        copy.start()
    fresh = [
        pltpu.make_async_copy(src, dst.at[pl.ds(8, 4)], lsem.at[8 + i])
        for i, (src, dst) in enumerate(
            ((f_cells_hbm, cells), (f_values_hbm, values), (f_weights_hbm, weights))
        )
    ]

    @pl.when(tm == n_tm - 1)
    def _():
        for copy in fresh:
            copy.start()

    barrier = pltpu.get_barrier_semaphore()
    greeted = 0
    for dt in (-1, 0, 1):
        for dl in (-1, 0, 1):
            if dt == 0 and dl == 0:
                continue
            ok = inside(dt, dl)

            @pl.when(ok)
            def _():
                pl.semaphore_signal(
                    barrier, inc=1, device_id=(tm + dt, lat + dl), device_id_type=MESH
                )

            greeted = greeted + ok.astype(jnp.int32)

    whole = slice(None)

    def blank(ref, *at):
        ref[at] = jnp.zeros(ref.at[at].shape, ref.dtype)

    @pl.when(lat == 0)
    def _():
        for r in range(4):
            blank(E, r, whole, slice(0, 8))
            blank(NX, r, whole, slice(0, 8))
        for k in range(3):
            blank(ND, k, whole, slice(0, 8))
        blank(NL, 0, whole, slice(0, 8))
        blank(XF, whole, slice(0, 48))
        blank(LF, whole, slice(0, 24))
        blank(RKX, whole, slice(0, 24))

    @pl.when(lat == n_lat - 1)
    def _():
        for r in range(4):
            blank(E, r, whole, slice(72, 80))
            blank(NX, r, whole, slice(72, 80))
        for k in range(3):
            blank(ND, k, whole, slice(72, 80))
        blank(NL, 0, whole, slice(72, 80))
        blank(XF, whole, slice(560, 608))
        blank(LF, whole, slice(536, 560))
        blank(RKX, whole, slice(280, 304))

    @pl.when(tm == 0)
    def _():
        blank(E, 0)
        blank(E, 1)

    @pl.when(tm == n_tm - 1)
    def _():
        for r in range(4):
            blank(NX, r)
        blank(NL, 0)
        blank(NL, 1)

    blank(XF, whole, slice(608, 640))
    blank(E, 2, whole, slice(72, 80))
    blank(LF, whole, slice(560, 576))

    def split(x):
        return jnp.stack([x[:, :half_lon], x[:, half_lon:]])

    def join(x):
        return jnp.concatenate([x[0], x[1]], axis=1)

    for copy in fetched[:5]:
        copy.wait()
    for s in range(8):
        XF[:, pl.ds(48 + s, 64, stride=8), :] = split(states[s])
        LF[:, pl.ds(24 + s, 64, stride=8), :] = split(mults[s])
    S7[0] = split(states[7])
    S0[0] = split(states[0])
    SL0[...] = split(mults[0])
    for k in range(3):
        ND[k, :, pl.ds(8, 64), :] = split(speeds[k])

    pl.semaphore_wait(barrier, greeted)

    def send_corners(r, before=True):
        moves = []
        if before:
            moves += [
                Move(S7.at[r, :, pl.ds(0, 8)], E.at[r, :, pl.ds(72, 8)], 1, -1),
                Move(S7.at[r, :, pl.ds(56, 8)], E.at[r, :, pl.ds(0, 8)], 1, 1),
            ]
        return moves + [
            Move(S0.at[r, :, pl.ds(0, 8)], NX.at[r, :, pl.ds(72, 8)], -1, -1),
            Move(S0.at[r, :, pl.ds(56, 8)], NX.at[r, :, pl.ds(0, 8)], -1, 1),
        ]

    def send_slots(r, before=True):
        moves = [Move(S7.at[r], E.at[r, :, pl.ds(8, 64)], 1, 0)] if before else []
        return moves + [Move(S0.at[r], NX.at[r, :, pl.ds(8, 64)], -1, 0)]

    def send_rows(r):
        return [
            Move(XF.at[:, pl.ds(48, 48)], HX.at[r, 1], 0, -1),
            Move(XF.at[:, pl.ds(512, 48)], HX.at[r, 0], 0, 1),
        ]

    def finish(moves):
        for move in moves:
            move.finish()

    def take_rows(r):
        @pl.when(lat > 0)
        def _():
            XF[:, pl.ds(0, 48), :] = HX[r, 0]

        @pl.when(lat < n_lat - 1)
        def _():
            XF[:, pl.ds(560, 48), :] = HX[r, 1]

    def edges(r):
        S7[r] = XF[:, pl.ds(55, 64, stride=8), :]
        S0[r] = XF[:, pl.ds(48, 64, stride=8), :]

    slot_moves = send_corners(0) + [
        Move(SL0.at[:, pl.ds(0, 8)], NL.at[0, :, pl.ds(72, 8)], -1, -1),
        Move(SL0.at[:, pl.ds(56, 8)], NL.at[0, :, pl.ds(0, 8)], -1, 1),
    ]
    row_moves = send_rows(0)
    row_moves += [
        Move(LF.at[:, pl.ds(24, 24)], HL.at[1], 0, -1),
        Move(LF.at[:, pl.ds(512, 24)], HL.at[0], 0, 1),
        Move(ND.at[:, :, pl.ds(8, 8)], ND.at[:, :, pl.ds(72, 8)], 0, -1),
        Move(ND.at[:, :, pl.ds(64, 8)], ND.at[:, :, pl.ds(0, 8)], 0, 1),
    ]
    slot_moves += send_slots(0) + [Move(SL0, NL.at[0, :, pl.ds(8, 64)], -1, 0)]
    for copy in fetched[5:]:
        copy.wait()
    obs_moves = [
        Move(cells.at[pl.ds(0, 4)], cells.at[pl.ds(8, 4)], -1, 0),
        Move(values.at[pl.ds(0, 4)], values.at[pl.ds(8, 4)], -1, 0),
        Move(weights.at[pl.ds(0, 4)], weights.at[pl.ds(8, 4)], -1, 0),
    ]

    n_obs = cells.shape[-1]

    def tables(c, y, w):
        row = lax.shift_right_logical(c, 8)
        column = lax.bitwise_and(c, 255)
        on_row = lax.broadcasted_iota(jnp.int32, (64, n_obs), 0) == row
        on_column = lax.broadcasted_iota(jnp.int32, (lon, n_obs), 0) == column
        wy = w * y
        parts = []
        for full in (w, wy):
            high = full.astype(jnp.bfloat16).astype(F32)
            for part in (high, full - high):
                parts.append(jnp.where(on_row, part, 0.0).astype(jnp.bfloat16))
        left = jnp.concatenate(parts, axis=0)
        right = jnp.where(on_column, 1.0, 0.0).astype(jnp.bfloat16)
        out = lax.dot_general(
            left, right, (((1,), (1,)), ((), ())), preferred_element_type=F32
        )
        return split(out[0:64] + out[64:128]), split(out[128:192] + out[192:256])

    def own_slot(s, carry):
        w, v = tables(cells[s], values[s], weights[s])
        WF[0, :, pl.ds(s, 64, stride=8), :] = w
        VF[0, :, pl.ds(s, 64, stride=8), :] = v
        return carry

    def kept_slot(s, carry):
        w, v = tables(cells[s + 4], values[s + 4], weights[s + 4])
        WF[0, :, pl.ds(s + 4, 64, stride=8), :] = w
        VF[0, :, pl.ds(s + 4, 64, stride=8), :] = v
        WF[1, :, pl.ds(s, 64, stride=8), :] = w
        VF[1, :, pl.ds(s, 64, stride=8), :] = v
        return carry

    def late_slot(s, carry):
        w, v = tables(cells[s + 8], values[s + 8], weights[s + 8])
        WF[1, :, pl.ds(s + 4, 64, stride=8), :] = w
        VF[1, :, pl.ds(s + 4, 64, stride=8), :] = v
        return carry

    lane = lax.broadcasted_iota(jnp.int32, (1, 1, half_lon), 2)

    def other(x):
        return jnp.stack([x[1], x[0]])

    def from_east(x):
        turned = pltpu.roll(x, half_lon - 1, 2)
        return jnp.where(lane == half_lon - 1, other(turned), turned)

    def from_west(x):
        turned = pltpu.roll(x, 1, 2)
        return jnp.where(lane == 0, other(turned), turned)

    def combine(first, count, kept):
        rows = pl.ds(first, count)
        d, u, v = ND[0, :, rows, :], 0.5 * ND[1, :, rows, :], 0.5 * ND[2, :, rows, :]
        row = lax.broadcasted_iota(jnp.int32, (2, count, half_lon), 1) + (first - 8) + lat * 64
        on_grid = jnp.logical_and(row >= 0, row < n_lat * 64)
        centre, north, south, east, west = 1.0 - 4.0 * d, d - v, d + v, d - u, d + u
        here = pl.ds(first + kept.start, kept.stop - kept.start)
        for k, value in enumerate((centre, north, south, east, west)):
            NF[k, :, here, :] = value[:, kept]
        adjoint = (
            centre,
            jnp.where(on_grid, pltpu.roll(south, count - 1, 1), 0.0),
            jnp.where(on_grid, pltpu.roll(north, 1, 1), 0.0),
            from_east(west),
            from_west(east),
        )
        for k, value in enumerate(adjoint):
            NB[k, :, here, :] = value[:, kept]

    def spread(first, count):
        def body(s, carry):
            for k in range(5):
                at = pl.ds(first * 8 + s, count, stride=8)
                CF[k, :, at, :] = NF[k, :, pl.ds(first, count), :]
                CB[k, :, at, :] = NB[k, :, pl.ds(first, count), :]
            return carry

        lax.fori_loop(0, 8, body, 0)

    def mix(c, mid, up, down):
        return (
            c[0] * mid
            + c[1] * up
            + c[2] * down
            + c[3] * from_east(mid)
            + c[4] * from_west(mid)
        )

    def tile(row, off):
        return pl.ds((row + off) * 8, 8)

    def one(src, off, coef, row):
        f = [src[:, tile(row + j, off), :] for j in (-1, 0, 1)]
        c = [coef[k, :, tile(row, 8), :] for k in range(5)]
        return mix(c, f[1], f[2], f[0])

    def over(rows, work):
        calc, store = work
        done = [calc(row) for row in rows]
        for row, value in zip(rows, done):
            store(row, value)

    def between(low, high, work):
        size = (high - low) // 2

        def step(i, carry):
            over([low + i * size + q for q in range(size)], work)
            return carry

        lax.fori_loop(0, 2, step, 0)

    def substep(src, off, coef, dst, dst_off):
        def store(row, value):
            dst[:, tile(row, dst_off), :] = value

        return (lambda row: one(src, off, coef, row)), store

    slot = lax.broadcasted_iota(jnp.int32, (1, 8, half_lon), 1)

    def cube(x):
        return x.reshape(2, x.shape[1] // 8, 8, half_lon)

    def flat(x):
        return x.reshape(2, x.shape[1] * 8, half_lon)

    def lone(field, coef, at, stride, levels):
        for level in range(levels):
            c = [
                [coef[k, :, pl.ds(at + level + 1 + q, 8, stride=stride), :] for k in range(5)]
                for q in range(len(field) - 2)
            ]
            field = [
                mix(c[q], field[q + 1], field[q + 2], field[q]) for q in range(len(field) - 2)
            ]
        return field

    def works(window):
        share = jnp.where(tm == 0, 0.0, 1.0) if window == 0 else 1.0

        def calc_jump(row):
            y = one(T2, 4, CF, row)
            x = XF[:, tile(row, 6), :]
            jump = jnp.where(slot > 0, x - pltpu.roll(y, 1, 1), share * x)
            return y, LF[:, tile(row, 3), :] + jump

        def store_jump(row, value):
            Y[:, tile(row, 3), :] = value[0]
            LF[:, tile(row, 3), :] = value[1]

        def calc_state(row):
            g = one(U2, 1, CB, row)
            g = jnp.where(slot < 7, pltpu.roll(g, 7, 1), 0.0)
            x = XF[:, tile(row, 6), :]
            p = LF[:, tile(row, 3), :]
            w = WF[window, :, tile(row, 0), :]
            y = VF[window, :, tile(row, 0), :]
            return x - STEP * (w * x - y + p - g)

        def store_state(row, value):
            XF[:, tile(row, 6), :] = value

        return (
            substep(XF, 6, CF, T1, 5),
            substep(T1, 5, CF, T2, 4),
            (calc_jump, store_jump),
            substep(LF, 3, CB, U1, 2),
            substep(U1, 2, CB, U2, 1),
            (calc_state, store_state),
        )

    def interior(window):
        for i, work in enumerate(works(window)):
            between(1 + i, 63 - i, work)

    def ends(window):
        for i, work in enumerate(works(window)):
            over([row for row in range(i - 5, i + 1)] + [row for row in range(63 - i, 69 - i)], work)

    def slots_beside(r, window):
        before = [E[r, :, pl.ds(2 + q, 8, stride=9), :] for q in range(15)]
        before = lone(before, NF, 2, 9, 3)
        after_on = jnp.where(tm == n_tm - 1, 0.0, 1.0)
        for q in range(9):
            jump = NX[r, :, pl.ds(5 + q, 8, stride=9), :]
            jump = jump - Y[:, pl.ds(q * 8 + 7, 8, stride=72), :]
            NL[window, :, pl.ds(5 + q, 8, stride=9), :] += after_on * jump
        after = [NL[window, :, pl.ds(5 + q, 8, stride=8), :] for q in range(14)]
        after = lone(after, NB, 5, 8, 3)
        for q in range(9):
            first = before[q]
            if window == 0:
                first = jnp.where(tm == 0, 0.0, 1.0) * first
            LF[:, pl.ds(q * 8, 8, stride=72), :] -= first
            XF[:, pl.ds((q + 3) * 8, 8, stride=72), :] += STEP * first
        for q in range(8):
            XF[:, pl.ds((q + 6) * 8 + 7, 8, stride=64), :] += STEP * after[q]

    low = lax.broadcasted_iota(jnp.int32, (1, 1, 8, half_lon), 2) < 4

    def pairs(v):
        return v.reshape(2, v.shape[1] // 16, 2, 8, half_lon)

    def pack(src, first, dst, at, count, size):
        def body(i, carry):
            v = pairs(src[:, pl.ds((first + i * size * 2) * 8, size * 16), :])
            v = jnp.where(low, v[:, :, 0], pltpu.roll(v[:, :, 1], 4, 2))
            dst[:, pl.ds((at + i * size) * 8, size * 8), :] = flat(v)
            return carry

        lax.fori_loop(0, count // size, body, 0)

    def unpack(src, dst, first, count, size, fill):
        def body(i, carry):
            at = first + i * size
            v = pairs(dst[:, pl.ds(at * 16, size * 16), :])
            p = cube(src[:, pl.ds(at * 8, size * 8), :])
            out = []
            for half, q in ((v[:, :, 0], pltpu.roll(p, 4, 2)), (v[:, :, 1], p)):
                q = jnp.where(tm == n_tm - 1, fill(half), q)
                out.append(jnp.where(low, pltpu.roll(half, 4, 2), q))
            out = jnp.stack(out, axis=2)
            dst[:, pl.ds(at * 16, size * 16), :] = out.reshape(2, size * 16, half_lon)
            return carry

        lax.fori_loop(0, count // size, body, 0)

    combine(8, 64, slice(0, 64))
    spread(8, 64)
    lax.fori_loop(0, 4, own_slot, 0)
    lax.fori_loop(0, 4, kept_slot, 0)
    interior(0)
    finish(row_moves)
    take_rows(0)

    @pl.when(lat > 0)
    def _():
        LF[:, pl.ds(0, 24), :] = HL[0]

    @pl.when(lat < n_lat - 1)
    def _():
        LF[:, pl.ds(536, 24), :] = HL[1]

    combine(0, 24, slice(0, 16))
    combine(56, 24, slice(8, 24))
    spread(0, 16)
    spread(64, 16)
    ends(0)
    finish(slot_moves)
    slots_beside(0, 0)
    edges(1)
    slot_moves = send_corners(1)
    row_moves = send_rows(1)
    slot_moves += send_slots(1)
    interior(0)
    pack(XF, 12, PKX, 3, 26, 13)
    pack(LF, 6, PKL, 3, 29, 29)
    early = [
        Move(PKX.at[:, pl.ds(24, 208)], RKX.at[:, pl.ds(48, 208)], -1, 0),
        Move(PKL.at[:, pl.ds(24, 232)], RKL.at[:, pl.ds(24, 232)], -1, 0),
    ]
    finish(obs_moves)

    @pl.when(tm == n_tm - 1)
    def _():
        for copy in fresh:
            copy.wait()

    lax.fori_loop(0, 4, late_slot, 0)
    finish(slot_moves)
    finish(row_moves)
    take_rows(1)
    ends(0)
    slots_beside(1, 0)

    row_moves = send_rows(2)
    pack(XF, 6, PKX, 0, 3, 3)
    pack(XF, 64, PKX, 29, 3, 3)
    S0[2] = XF[:, pl.ds(52, 64, stride=8), :]
    slot_moves = send_corners(2, before=False)
    corner_moves = [
        Move(PKX.at[:, pl.ds(0, 24)], RKX.at[:, pl.ds(280, 24)], -1, -1),
        Move(PKX.at[:, pl.ds(232, 24)], RKX.at[:, pl.ds(0, 24)], -1, 1),
    ]
    pack(LF, 0, PKL, 0, 3, 3)
    pack(LF, 64, PKL, 32, 3, 3)
    SXZ[...] = XF[:, pl.ds(48, 64, stride=8), :]
    SLZ[:, pl.ds(0, 70), :] = LF[:, pl.ds(0, 70, stride=8), :]
    slab_moves = [
        Move(PKL.at[:, pl.ds(0, 24)], RKL.at[:, pl.ds(0, 24)], -1, 0),
        Move(PKL.at[:, pl.ds(256, 24)], RKL.at[:, pl.ds(256, 24)], -1, 0),
        Move(SLZ, RLZ, -1, 0),
        Move(PKX.at[:, pl.ds(0, 24)], RKX.at[:, pl.ds(24, 24)], -1, 0),
        Move(PKX.at[:, pl.ds(232, 24)], RKX.at[:, pl.ds(256, 24)], -1, 0),
        Move(SXZ, RXZ, -1, 0),
    ]
    SL4[:, pl.ds(5, 70), :] = LF[:, pl.ds(4, 70, stride=8), :]
    slot_moves += send_slots(2, before=False)
    slot_moves.append(Move(SL4, NL.at[1], -1, 0))
    E[2, :, pl.ds(8, 64), :] = XF[:, pl.ds(51, 64, stride=8), :]

    def repeat(half):
        return jnp.broadcast_to(half[:, :, 7:8], half.shape)

    finish(early)
    finish(slab_moves)
    unpack(RKL, LF, 0, 35, 5, jnp.zeros_like)
    for move in row_moves:
        move.sent()
    unpack(RKX, XF, 3, 32, 8, repeat)

    @pl.when(tm < n_tm - 1)
    def _():
        XF[:, pl.ds(52, 64, stride=8), :] = RXZ[...]
        LF[:, pl.ds(4, 70, stride=8), :] = RLZ[:, pl.ds(0, 70), :]

    interior(1)
    finish(row_moves)
    take_rows(2)
    E[2, :, pl.ds(2, 6), :] = XF[:, pl.ds(3, 6, stride=8), :]
    E[2, :, pl.ds(72, 6), :] = XF[:, pl.ds(563, 6, stride=8), :]
    finish(slot_moves)
    finish(corner_moves)
    unpack(RKX, XF, 0, 3, 3, repeat)
    unpack(RKX, XF, 35, 3, 3, repeat)
    ends(1)
    slots_beside(2, 1)
    edges(3)
    slot_moves = send_corners(3)
    row_moves = send_rows(3)
    slot_moves += send_slots(3)

    @pl.when(tm == 0)
    def _():
        E[3] = E[2]

    interior(1)
    finish(slot_moves)
    finish(row_moves)
    take_rows(3)
    ends(1)
    slots_beside(3, 1)
    results = [
        pltpu.make_async_copy(XF.at[:, pl.ds(48, 512)], x_out, lsem.at[0]),
        pltpu.make_async_copy(LF.at[:, pl.ds(24, 512)], l_out, lsem.at[1]),
    ]
    for copy in results:
        copy.start()
    for copy in results:
        copy.wait()
    assert made[0] == n_transfers


def unweave(x_hbm, l_hbm, x_out, l_out, x_ref, l_ref, sems):
    copies = [
        pltpu.make_async_copy(src, dst, sems.at[i])
        for i, (src, dst) in enumerate(((x_hbm, x_ref), (l_hbm, l_ref)))
    ]
    for copy in copies:
        copy.start()
    for copy, ref, out in zip(copies, (x_ref, l_ref), (x_out, l_out)):
        copy.wait()
        for s in range(8):
            x = ref[:, pl.ds(s, 64, stride=8), :]
            out[s] = jnp.concatenate([x[0], x[1]], axis=1)


def body(n_tm, n_lat, *arrays):
    states = arrays[0]
    slots, rows, lon = states.shape
    n_obs = arrays[5].shape[-1]
    n_transfers = 50

    def vmem(*shape, kind=F32):
        return pltpu.VMEM(shape, kind)

    woven = jax.ShapeDtypeStruct((2, slots * rows, lon // 2), F32)
    shape = jax.ShapeDtypeStruct((slots, rows, lon), F32)
    fields = pl.pallas_call(
        functools.partial(weave, n_tm, n_lat, n_transfers),
        out_shape=(woven, woven),
        in_specs=[pl.BlockSpec(memory_space=pltpu.HBM)] * len(arrays),
        out_specs=(pl.BlockSpec(memory_space=pltpu.HBM),) * 2,
        scratch_shapes=[
            vmem(2, 640, lon // 2),
            vmem(2, 576, lon // 2),
            vmem(2, 592, lon // 2),
            vmem(2, 576, lon // 2),
            vmem(2, 576, lon // 2),
            vmem(2, 544, lon // 2),
            vmem(2, 528, lon // 2),
            vmem(5, 2, 640, lon // 2),
            vmem(5, 2, 640, lon // 2),
            vmem(3, 2, 80, lon // 2),
            vmem(5, 2, 80, lon // 2),
            vmem(5, 2, 80, lon // 2),
            vmem(2, 2, 512, lon // 2),
            vmem(2, 2, 512, lon // 2),
            vmem(4, 2, 2, 48, lon // 2),
            vmem(2, 2, 24, lon // 2),
            vmem(4, 2, 80, lon // 2),
            vmem(4, 2, 80, lon // 2),
            vmem(2, 2, 80, lon // 2),
            vmem(4, 2, 64, lon // 2),
            vmem(4, 2, 64, lon // 2),
            vmem(2, 64, lon // 2),
            vmem(2, 256, lon // 2),
            vmem(2, 280, lon // 2),
            vmem(2, 80, lon // 2),
            vmem(2, 304, lon // 2),
            vmem(2, 280, lon // 2),
            vmem(2, 64, lon // 2),
            vmem(2, 72, lon // 2),
            vmem(2, 64, lon // 2),
            vmem(2, 72, lon // 2),
            vmem(slots, rows, lon),
            vmem(slots, rows, lon),
            vmem(3, rows, lon),
            vmem(12, 1, n_obs, kind=jnp.int32),
            vmem(12, 1, n_obs),
            vmem(12, 1, n_obs),
            pltpu.SemaphoreType.DMA((n_transfers,)),
            pltpu.SemaphoreType.DMA((n_transfers,)),
            pltpu.SemaphoreType.DMA((11,)),
        ],
        compiler_params=pltpu.CompilerParams(
            collective_id=0, has_side_effects=True, vmem_limit_bytes=64 * 1024 * 1024 - 65536
        ),
    )(*arrays)
    return pl.pallas_call(
        unweave,
        out_shape=(shape, shape),
        in_specs=[pl.BlockSpec(memory_space=pltpu.HBM)] * 2,
        out_specs=(pl.BlockSpec(memory_space=pltpu.VMEM),) * 2,
        scratch_shapes=[
            vmem(2, 512, lon // 2),
            vmem(2, 512, lon // 2),
            pltpu.SemaphoreType.DMA((2,)),
        ],
        compiler_params=pltpu.CompilerParams(vmem_limit_bytes=64 * 1024 * 1024 - 65536),
    )(*fields)


def solution(mesh):
    field = P("tm", "lat", None)
    plane = P("lat", None)
    fresh = P(None, "lat", None)
    in_specs = (field, field, plane, plane, plane, field, field, field, fresh, fresh, fresh)
    return jax.shard_map(
        functools.partial(body, mesh.shape["tm"], mesh.shape["lat"]),
        mesh=mesh,
        in_specs=in_specs,
        out_specs=(field, field),
        check_vma=False,
    )
```

```python
import functools

import jax
import jax.numpy as jnp
from jax import lax
from jax.experimental import pallas as pl
from jax.experimental.pallas import tpu as pltpu
from jax.sharding import PartitionSpec as P

MESH = pl.DeviceIdType.MESH
STEP = 0.15
F32 = jnp.float32


def weave(n_tm, n_lat, n_transfers, *refs):
    (
        states_hbm,
        mults_hbm,
        diff_hbm,
        zonal_hbm,
        merid_hbm,
        cells_hbm,
        values_hbm,
        weights_hbm,
        f_cells_hbm,
        f_values_hbm,
        f_weights_hbm,
        x_out,
        l_out,
        XF,
        LF,
        T1,
        T2,
        Y,
        U1,
        U2,
        CF,
        CB,
        ND,
        NF,
        NB,
        WF,
        VF,
        HX,
        HL,
        E,
        NX,
        NL,
        S7,
        S0,
        SL0,
        PKX,
        PKL,
        SL4,
        RKX,
        RKL,
        SXZ,
        SLZ,
        RXZ,
        RLZ,
        states,
        mults,
        speeds,
        cells,
        values,
        weights,
        ssem,
        rsem,
        lsem,
    ) = refs
    lon = 2 * XF.shape[-1]
    half_lon = lon // 2
    tm = lax.axis_index("tm")
    lat = lax.axis_index("lat")
    made = [0]

    def inside(dt, dl):
        ok = True
        if dt > 0:
            ok = tm < n_tm - 1
        elif dt < 0:
            ok = tm > 0
        if dl > 0:
            ok = jnp.logical_and(ok, lat < n_lat - 1)
        elif dl < 0:
            ok = jnp.logical_and(ok, lat > 0)
        return ok

    class Move:
        def __init__(self, src, dst, dt, dl):
            i = made[0]
            made[0] += 1
            assert i < n_transfers
            self.to, self.by = inside(dt, dl), inside(-dt, -dl)
            self.copy = pltpu.make_async_remote_copy(
                src_ref=src,
                dst_ref=dst,
                send_sem=ssem.at[i],
                recv_sem=rsem.at[i],
                device_id=(tm + dt, lat + dl),
                device_id_type=MESH,
            )
            pl.when(self.to)(self.copy.start)

        def sent(self):
            pl.when(self.to)(self.copy.wait_send)
            self.to = None

        def finish(self):
            if self.to is not None:
                self.sent()
            pl.when(self.by)(self.copy.wait_recv)

    fetched = [
        pltpu.make_async_copy(src, dst, lsem.at[i])
        for i, (src, dst) in enumerate(
            (
                (states_hbm, states),
                (mults_hbm, mults),
                (diff_hbm, speeds.at[0]),
                (zonal_hbm, speeds.at[1]),
                (merid_hbm, speeds.at[2]),
                (cells_hbm, cells.at[pl.ds(0, 8)]),
                (values_hbm, values.at[pl.ds(0, 8)]),
                (weights_hbm, weights.at[pl.ds(0, 8)]),
            )
        )
    ]
    for copy in fetched:
        copy.start()
    fresh = [
        pltpu.make_async_copy(src, dst.at[pl.ds(8, 4)], lsem.at[8 + i])
        for i, (src, dst) in enumerate(
            ((f_cells_hbm, cells), (f_values_hbm, values), (f_weights_hbm, weights))
        )
    ]

    @pl.when(tm == n_tm - 1)
    def _():
        for copy in fresh:
            copy.start()

    barrier = pltpu.get_barrier_semaphore()
    greeted = 0
    for dt in (-1, 0, 1):
        for dl in (-1, 0, 1):
            if dt == 0 and dl == 0:
                continue
            ok = inside(dt, dl)

            @pl.when(ok)
            def _():
                pl.semaphore_signal(
                    barrier, inc=1, device_id=(tm + dt, lat + dl), device_id_type=MESH
                )

            greeted = greeted + ok.astype(jnp.int32)

    whole = slice(None)

    def blank(ref, *at):
        ref[at] = jnp.zeros(ref.at[at].shape, ref.dtype)

    @pl.when(lat == 0)
    def _():
        for r in range(4):
            blank(E, r, whole, slice(0, 8))
            blank(NX, r, whole, slice(0, 8))
        for k in range(3):
            blank(ND, k, whole, slice(0, 8))
        blank(NL, 0, whole, slice(0, 8))
        blank(XF, whole, slice(0, 48))
        blank(LF, whole, slice(0, 24))
        blank(RKX, whole, slice(0, 24))

    @pl.when(lat == n_lat - 1)
    def _():
        for r in range(4):
            blank(E, r, whole, slice(72, 80))
            blank(NX, r, whole, slice(72, 80))
        for k in range(3):
            blank(ND, k, whole, slice(72, 80))
        blank(NL, 0, whole, slice(72, 80))
        blank(XF, whole, slice(560, 608))
        blank(LF, whole, slice(536, 560))
        blank(RKX, whole, slice(280, 304))

    @pl.when(tm == 0)
    def _():
        blank(E, 0)
        blank(E, 1)

    @pl.when(tm == n_tm - 1)
    def _():
        for r in range(4):
            blank(NX, r)
        blank(NL, 0)
        blank(NL, 1)

    blank(XF, whole, slice(608, 640))
    blank(E, 2, whole, slice(72, 80))
    blank(LF, whole, slice(560, 576))

    def split(x):
        return jnp.stack([x[:, :half_lon], x[:, half_lon:]])

    def join(x):
        return jnp.concatenate([x[0], x[1]], axis=1)

    for copy in fetched[:5]:
        copy.wait()
    for s in range(8):
        XF[:, pl.ds(48 + s, 64, stride=8), :] = split(states[s])
        LF[:, pl.ds(24 + s, 64, stride=8), :] = split(mults[s])
    S7[0] = split(states[7])
    S0[0] = split(states[0])
    SL0[...] = split(mults[0])
    for k in range(3):
        ND[k, :, pl.ds(8, 64), :] = split(speeds[k])

    pl.semaphore_wait(barrier, greeted)

    def send_corners(r, before=True):
        moves = []
        if before:
            moves += [
                Move(S7.at[r, :, pl.ds(0, 8)], E.at[r, :, pl.ds(72, 8)], 1, -1),
                Move(S7.at[r, :, pl.ds(56, 8)], E.at[r, :, pl.ds(0, 8)], 1, 1),
            ]
        return moves + [
            Move(S0.at[r, :, pl.ds(0, 8)], NX.at[r, :, pl.ds(72, 8)], -1, -1),
            Move(S0.at[r, :, pl.ds(56, 8)], NX.at[r, :, pl.ds(0, 8)], -1, 1),
        ]

    def send_slots(r, before=True):
        moves = [Move(S7.at[r], E.at[r, :, pl.ds(8, 64)], 1, 0)] if before else []
        return moves + [Move(S0.at[r], NX.at[r, :, pl.ds(8, 64)], -1, 0)]

    def send_rows(r):
        return [
            Move(XF.at[:, pl.ds(48, 48)], HX.at[r, 1], 0, -1),
            Move(XF.at[:, pl.ds(512, 48)], HX.at[r, 0], 0, 1),
        ]

    def finish(moves):
        for move in moves:
            move.finish()

    def take_rows(r):
        @pl.when(lat > 0)
        def _():
            XF[:, pl.ds(0, 48), :] = HX[r, 0]

        @pl.when(lat < n_lat - 1)
        def _():
            XF[:, pl.ds(560, 48), :] = HX[r, 1]

    def edges(r):
        S7[r] = XF[:, pl.ds(55, 64, stride=8), :]
        S0[r] = XF[:, pl.ds(48, 64, stride=8), :]

    slot_moves = send_corners(0) + [
        Move(SL0.at[:, pl.ds(0, 8)], NL.at[0, :, pl.ds(72, 8)], -1, -1),
        Move(SL0.at[:, pl.ds(56, 8)], NL.at[0, :, pl.ds(0, 8)], -1, 1),
    ]
    row_moves = send_rows(0)
    row_moves += [
        Move(LF.at[:, pl.ds(24, 24)], HL.at[1], 0, -1),
        Move(LF.at[:, pl.ds(512, 24)], HL.at[0], 0, 1),
        Move(ND.at[:, :, pl.ds(8, 8)], ND.at[:, :, pl.ds(72, 8)], 0, -1),
        Move(ND.at[:, :, pl.ds(64, 8)], ND.at[:, :, pl.ds(0, 8)], 0, 1),
    ]
    slot_moves += send_slots(0) + [Move(SL0, NL.at[0, :, pl.ds(8, 64)], -1, 0)]
    for copy in fetched[5:]:
        copy.wait()
    obs_moves = [
        Move(cells.at[pl.ds(0, 4)], cells.at[pl.ds(8, 4)], -1, 0),
        Move(values.at[pl.ds(0, 4)], values.at[pl.ds(8, 4)], -1, 0),
        Move(weights.at[pl.ds(0, 4)], weights.at[pl.ds(8, 4)], -1, 0),
    ]

    n_obs = cells.shape[-1]

    def tables(c, y, w):
        row = lax.shift_right_logical(c, 8)
        column = lax.bitwise_and(c, 255)
        on_row = lax.broadcasted_iota(jnp.int32, (64, n_obs), 0) == row
        on_column = lax.broadcasted_iota(jnp.int32, (lon, n_obs), 0) == column
        wy = w * y
        parts = []
        for full in (w, wy):
            high = full.astype(jnp.bfloat16).astype(F32)
            for part in (high, full - high):
                parts.append(jnp.where(on_row, part, 0.0).astype(jnp.bfloat16))
        left = jnp.concatenate(parts, axis=0)
        right = jnp.where(on_column, 1.0, 0.0).astype(jnp.bfloat16)
        out = lax.dot_general(
            left, right, (((1,), (1,)), ((), ())), preferred_element_type=F32
        )
        return split(out[0:64] + out[64:128]), split(out[128:192] + out[192:256])

    def own_slot(s, carry):
        w, v = tables(cells[s], values[s], weights[s])
        WF[0, :, pl.ds(s, 64, stride=8), :] = w
        VF[0, :, pl.ds(s, 64, stride=8), :] = v
        return carry

    def kept_slot(s, carry):
        w, v = tables(cells[s + 4], values[s + 4], weights[s + 4])
        WF[0, :, pl.ds(s + 4, 64, stride=8), :] = w
        VF[0, :, pl.ds(s + 4, 64, stride=8), :] = v
        WF[1, :, pl.ds(s, 64, stride=8), :] = w
        VF[1, :, pl.ds(s, 64, stride=8), :] = v
        return carry

    def late_slot(s, carry):
        w, v = tables(cells[s + 8], values[s + 8], weights[s + 8])
        WF[1, :, pl.ds(s + 4, 64, stride=8), :] = w
        VF[1, :, pl.ds(s + 4, 64, stride=8), :] = v
        return carry

    lane = lax.broadcasted_iota(jnp.int32, (1, 1, half_lon), 2)

    def other(x):
        return jnp.stack([x[1], x[0]])

    def from_east(x):
        turned = pltpu.roll(x, half_lon - 1, 2)
        return jnp.where(lane == half_lon - 1, other(turned), turned)

    def from_west(x):
        turned = pltpu.roll(x, 1, 2)
        return jnp.where(lane == 0, other(turned), turned)

    def combine(first, count, kept):
        rows = pl.ds(first, count)
        d, u, v = ND[0, :, rows, :], 0.5 * ND[1, :, rows, :], 0.5 * ND[2, :, rows, :]
        row = lax.broadcasted_iota(jnp.int32, (2, count, half_lon), 1) + (first - 8) + lat * 64
        on_grid = jnp.logical_and(row >= 0, row < n_lat * 64)
        centre, north, south, east, west = 1.0 - 4.0 * d, d - v, d + v, d - u, d + u
        here = pl.ds(first + kept.start, kept.stop - kept.start)
        for k, value in enumerate((centre, north, south, east, west)):
            NF[k, :, here, :] = value[:, kept]
        adjoint = (
            centre,
            jnp.where(on_grid, pltpu.roll(south, count - 1, 1), 0.0),
            jnp.where(on_grid, pltpu.roll(north, 1, 1), 0.0),
            from_east(west),
            from_west(east),
        )
        for k, value in enumerate(adjoint):
            NB[k, :, here, :] = value[:, kept]

    def spread(first, count):
        def body(s, carry):
            for k in range(5):
                at = pl.ds(first * 8 + s, count, stride=8)
                CF[k, :, at, :] = NF[k, :, pl.ds(first, count), :]
                CB[k, :, at, :] = NB[k, :, pl.ds(first, count), :]
            return carry

        lax.fori_loop(0, 8, body, 0)

    def mix(c, mid, up, down):
        return (
            c[0] * mid
            + c[1] * up
            + c[2] * down
            + c[3] * from_east(mid)
            + c[4] * from_west(mid)
        )

    def tile(row, off):
        return pl.ds((row + off) * 8, 8)

    def one(src, off, coef, row):
        f = [src[:, tile(row + j, off), :] for j in (-1, 0, 1)]
        c = [coef[k, :, tile(row, 8), :] for k in range(5)]
        return mix(c, f[1], f[2], f[0])

    def over(rows, work):
        calc, store = work
        done = [calc(row) for row in rows]
        for row, value in zip(rows, done):
            store(row, value)

    def between(low, high, work):
        size = (high - low) // 2

        def step(i, carry):
            over([low + i * size + q for q in range(size)], work)
            return carry

        lax.fori_loop(0, 2, step, 0)

    def substep(src, off, coef, dst, dst_off):
        def store(row, value):
            dst[:, tile(row, dst_off), :] = value

        return (lambda row: one(src, off, coef, row)), store

    slot = lax.broadcasted_iota(jnp.int32, (1, 8, half_lon), 1)

    def cube(x):
        return x.reshape(2, x.shape[1] // 8, 8, half_lon)

    def flat(x):
        return x.reshape(2, x.shape[1] * 8, half_lon)

    def lone(field, coef, at, stride, levels):
        for level in range(levels):
            c = [
                [coef[k, :, pl.ds(at + level + 1 + q, 8, stride=stride), :] for k in range(5)]
                for q in range(len(field) - 2)
            ]
            field = [
                mix(c[q], field[q + 1], field[q + 2], field[q]) for q in range(len(field) - 2)
            ]
        return field

    def works(window):
        share = jnp.where(tm == 0, 0.0, 1.0) if window == 0 else 1.0

        def calc_jump(row):
            y = one(T2, 4, CF, row)
            x = XF[:, tile(row, 6), :]
            jump = jnp.where(slot > 0, x - pltpu.roll(y, 1, 1), share * x)
            return y, LF[:, tile(row, 3), :] + jump

        def store_jump(row, value):
            Y[:, tile(row, 3), :] = value[0]
            LF[:, tile(row, 3), :] = value[1]

        def calc_state(row):
            g = one(U2, 1, CB, row)
            g = jnp.where(slot < 7, pltpu.roll(g, 7, 1), 0.0)
            x = XF[:, tile(row, 6), :]
            p = LF[:, tile(row, 3), :]
            w = WF[window, :, tile(row, 0), :]
            y = VF[window, :, tile(row, 0), :]
            return x - STEP * (w * x - y + p - g)

        def store_state(row, value):
            XF[:, tile(row, 6), :] = value

        return (
            substep(XF, 6, CF, T1, 5),
            substep(T1, 5, CF, T2, 4),
            (calc_jump, store_jump),
            substep(LF, 3, CB, U1, 2),
            substep(U1, 2, CB, U2, 1),
            (calc_state, store_state),
        )

    def interior(window):
        for i, work in enumerate(works(window)):
            between(1 + i, 63 - i, work)

    def ends(window):
        for i, work in enumerate(works(window)):
            over([row for row in range(i - 5, i + 1)] + [row for row in range(63 - i, 69 - i)], work)

    def slots_beside(r, window):
        before = [E[r, :, pl.ds(2 + q, 8, stride=9), :] for q in range(15)]
        before = lone(before, NF, 2, 9, 3)
        after_on = jnp.where(tm == n_tm - 1, 0.0, 1.0)
        for q in range(9):
            jump = NX[r, :, pl.ds(5 + q, 8, stride=9), :]
            jump = jump - Y[:, pl.ds(q * 8 + 7, 8, stride=72), :]
            NL[window, :, pl.ds(5 + q, 8, stride=9), :] += after_on * jump
        after = [NL[window, :, pl.ds(5 + q, 8, stride=8), :] for q in range(14)]
        after = lone(after, NB, 5, 8, 3)
        for q in range(9):
            first = before[q]
            if window == 0:
                first = jnp.where(tm == 0, 0.0, 1.0) * first
            LF[:, pl.ds(q * 8, 8, stride=72), :] -= first
            XF[:, pl.ds((q + 3) * 8, 8, stride=72), :] += STEP * first
        for q in range(8):
            XF[:, pl.ds((q + 6) * 8 + 7, 8, stride=64), :] += STEP * after[q]

    low = lax.broadcasted_iota(jnp.int32, (1, 1, 8, half_lon), 2) < 4

    def pairs(v):
        return v.reshape(2, v.shape[1] // 16, 2, 8, half_lon)

    def pack(src, first, dst, at, count, size):
        def body(i, carry):
            v = pairs(src[:, pl.ds((first + i * size * 2) * 8, size * 16), :])
            v = jnp.where(low, v[:, :, 0], pltpu.roll(v[:, :, 1], 4, 2))
            dst[:, pl.ds((at + i * size) * 8, size * 8), :] = flat(v)
            return carry

        lax.fori_loop(0, count // size, body, 0)

    def unpack(src, dst, first, count, size, fill):
        def body(i, carry):
            at = first + i * size
            v = pairs(dst[:, pl.ds(at * 16, size * 16), :])
            p = cube(src[:, pl.ds(at * 8, size * 8), :])
            out = []
            for half, q in ((v[:, :, 0], pltpu.roll(p, 4, 2)), (v[:, :, 1], p)):
                q = jnp.where(tm == n_tm - 1, fill(half), q)
                out.append(jnp.where(low, pltpu.roll(half, 4, 2), q))
            out = jnp.stack(out, axis=2)
            dst[:, pl.ds(at * 16, size * 16), :] = out.reshape(2, size * 16, half_lon)
            return carry

        lax.fori_loop(0, count // size, body, 0)

    combine(8, 64, slice(0, 64))
    spread(8, 64)
    lax.fori_loop(0, 4, own_slot, 0)
    lax.fori_loop(0, 4, kept_slot, 0)
    interior(0)
    finish(row_moves)
    take_rows(0)

    @pl.when(lat > 0)
    def _():
        LF[:, pl.ds(0, 24), :] = HL[0]

    @pl.when(lat < n_lat - 1)
    def _():
        LF[:, pl.ds(536, 24), :] = HL[1]

    combine(0, 24, slice(0, 16))
    combine(56, 24, slice(8, 24))
    spread(0, 16)
    spread(64, 16)
    ends(0)
    finish(slot_moves)
    slots_beside(0, 0)
    edges(1)
    slot_moves = send_corners(1)
    row_moves = send_rows(1)
    slot_moves += send_slots(1)
    interior(0)
    pack(XF, 12, PKX, 3, 26, 13)
    pack(LF, 6, PKL, 3, 29, 29)
    early = [
        Move(PKX.at[:, pl.ds(24, 208)], RKX.at[:, pl.ds(48, 208)], -1, 0),
        Move(PKL.at[:, pl.ds(24, 232)], RKL.at[:, pl.ds(24, 232)], -1, 0),
    ]
    finish(obs_moves)

    @pl.when(tm == n_tm - 1)
    def _():
        for copy in fresh:
            copy.wait()

    lax.fori_loop(0, 4, late_slot, 0)
    finish(slot_moves)
    finish(row_moves)
    take_rows(1)
    ends(0)
    slots_beside(1, 0)

    row_moves = send_rows(2)
    pack(XF, 6, PKX, 0, 3, 3)
    pack(XF, 64, PKX, 29, 3, 3)
    S0[2] = XF[:, pl.ds(52, 64, stride=8), :]
    slot_moves = send_corners(2, before=False)
    corner_moves = [
        Move(PKX.at[:, pl.ds(0, 24)], RKX.at[:, pl.ds(280, 24)], -1, -1),
        Move(PKX.at[:, pl.ds(232, 24)], RKX.at[:, pl.ds(0, 24)], -1, 1),
    ]
    pack(LF, 0, PKL, 0, 3, 3)
    pack(LF, 64, PKL, 32, 3, 3)
    SXZ[...] = XF[:, pl.ds(48, 64, stride=8), :]
    SLZ[:, pl.ds(0, 70), :] = LF[:, pl.ds(0, 70, stride=8), :]
    slab_moves = [
        Move(PKL.at[:, pl.ds(0, 24)], RKL.at[:, pl.ds(0, 24)], -1, 0),
        Move(PKL.at[:, pl.ds(256, 24)], RKL.at[:, pl.ds(256, 24)], -1, 0),
        Move(SLZ, RLZ, -1, 0),
        Move(PKX.at[:, pl.ds(0, 24)], RKX.at[:, pl.ds(24, 24)], -1, 0),
        Move(PKX.at[:, pl.ds(232, 24)], RKX.at[:, pl.ds(256, 24)], -1, 0),
        Move(SXZ, RXZ, -1, 0),
    ]
    SL4[:, pl.ds(5, 70), :] = LF[:, pl.ds(4, 70, stride=8), :]
    slot_moves += send_slots(2, before=False)
    slot_moves.append(Move(SL4, NL.at[1], -1, 0))
    E[2, :, pl.ds(8, 64), :] = XF[:, pl.ds(51, 64, stride=8), :]

    def repeat(half):
        return jnp.broadcast_to(half[:, :, 7:8], half.shape)

    finish(early)
    finish(slab_moves)
    unpack(RKL, LF, 0, 35, 5, jnp.zeros_like)
    for move in row_moves:
        move.sent()
    unpack(RKX, XF, 3, 32, 8, repeat)

    @pl.when(tm < n_tm - 1)
    def _():
        XF[:, pl.ds(52, 64, stride=8), :] = RXZ[...]
        LF[:, pl.ds(4, 70, stride=8), :] = RLZ[:, pl.ds(0, 70), :]

    interior(1)
    finish(row_moves)
    take_rows(2)
    E[2, :, pl.ds(2, 6), :] = XF[:, pl.ds(3, 6, stride=8), :]
    E[2, :, pl.ds(72, 6), :] = XF[:, pl.ds(563, 6, stride=8), :]
    finish(slot_moves)
    finish(corner_moves)
    unpack(RKX, XF, 0, 3, 3, repeat)
    unpack(RKX, XF, 35, 3, 3, repeat)
    ends(1)
    slots_beside(2, 1)
    edges(3)
    slot_moves = send_corners(3)
    row_moves = send_rows(3)
    slot_moves += send_slots(3)

    @pl.when(tm == 0)
    def _():
        E[3] = E[2]

    interior(1)
    finish(slot_moves)
    finish(row_moves)
    take_rows(3)
    ends(1)
    slots_beside(3, 1)
    results = [
        pltpu.make_async_copy(XF.at[:, pl.ds(48, 512)], x_out, lsem.at[0]),
        pltpu.make_async_copy(LF.at[:, pl.ds(24, 512)], l_out, lsem.at[1]),
    ]
    for copy in results:
        copy.start()
    for copy in results:
        copy.wait()
    assert made[0] == n_transfers


def unweave(x_hbm, l_hbm, x_out, l_out, x_ref, l_ref, x_laid, l_laid, sems):
    refs = ((x_hbm, x_ref, x_laid, x_out), (l_hbm, l_ref, l_laid, l_out))
    arriving = [
        pltpu.make_async_copy(refs[i][0], refs[i][1], sems.at[i]) for i in range(2)
    ]
    for copy in arriving:
        copy.start()
    leaving = []
    for i, (_, ref, laid, out) in enumerate(refs):
        arriving[i].wait()
        for s in range(8):
            x = ref[:, pl.ds(s, 64, stride=8), :]
            laid[s] = jnp.concatenate([x[0], x[1]], axis=1)
        leaving.append(pltpu.make_async_copy(laid, out, sems.at[2 + i]))
        leaving[i].start()
    for copy in leaving:
        copy.wait()


def body(n_tm, n_lat, *arrays):
    states = arrays[0]
    slots, rows, lon = states.shape
    n_obs = arrays[5].shape[-1]
    n_transfers = 50

    def vmem(*shape, kind=F32):
        return pltpu.VMEM(shape, kind)

    woven = jax.ShapeDtypeStruct((2, slots * rows, lon // 2), F32)
    shape = jax.ShapeDtypeStruct((slots, rows, lon), F32)
    fields = pl.pallas_call(
        functools.partial(weave, n_tm, n_lat, n_transfers),
        out_shape=(woven, woven),
        in_specs=[pl.BlockSpec(memory_space=pltpu.HBM)] * len(arrays),
        out_specs=(pl.BlockSpec(memory_space=pltpu.HBM),) * 2,
        scratch_shapes=[
            vmem(2, 640, lon // 2),
            vmem(2, 576, lon // 2),
            vmem(2, 592, lon // 2),
            vmem(2, 576, lon // 2),
            vmem(2, 576, lon // 2),
            vmem(2, 544, lon // 2),
            vmem(2, 528, lon // 2),
            vmem(5, 2, 640, lon // 2),
            vmem(5, 2, 640, lon // 2),
            vmem(3, 2, 80, lon // 2),
            vmem(5, 2, 80, lon // 2),
            vmem(5, 2, 80, lon // 2),
            vmem(2, 2, 512, lon // 2),
            vmem(2, 2, 512, lon // 2),
            vmem(4, 2, 2, 48, lon // 2),
            vmem(2, 2, 24, lon // 2),
            vmem(4, 2, 80, lon // 2),
            vmem(4, 2, 80, lon // 2),
            vmem(2, 2, 80, lon // 2),
            vmem(4, 2, 64, lon // 2),
            vmem(4, 2, 64, lon // 2),
            vmem(2, 64, lon // 2),
            vmem(2, 256, lon // 2),
            vmem(2, 280, lon // 2),
            vmem(2, 80, lon // 2),
            vmem(2, 304, lon // 2),
            vmem(2, 280, lon // 2),
            vmem(2, 64, lon // 2),
            vmem(2, 72, lon // 2),
            vmem(2, 64, lon // 2),
            vmem(2, 72, lon // 2),
            vmem(slots, rows, lon),
            vmem(slots, rows, lon),
            vmem(3, rows, lon),
            vmem(12, 1, n_obs, kind=jnp.int32),
            vmem(12, 1, n_obs),
            vmem(12, 1, n_obs),
            pltpu.SemaphoreType.DMA((n_transfers,)),
            pltpu.SemaphoreType.DMA((n_transfers,)),
            pltpu.SemaphoreType.DMA((11,)),
        ],
        compiler_params=pltpu.CompilerParams(
            collective_id=0, has_side_effects=True, vmem_limit_bytes=64 * 1024 * 1024 - 65536
        ),
    )(*arrays)
    return pl.pallas_call(
        unweave,
        out_shape=(shape, shape),
        in_specs=[pl.BlockSpec(memory_space=pltpu.HBM)] * 2,
        out_specs=(pl.BlockSpec(memory_space=pltpu.HBM),) * 2,
        scratch_shapes=[
            vmem(2, 512, lon // 2),
            vmem(2, 512, lon // 2),
            vmem(slots, rows, lon),
            vmem(slots, rows, lon),
            pltpu.SemaphoreType.DMA((4,)),
        ],
        compiler_params=pltpu.CompilerParams(vmem_limit_bytes=64 * 1024 * 1024 - 65536),
    )(*fields)


def solution(mesh):
    field = P("tm", "lat", None)
    plane = P("lat", None)
    fresh = P(None, "lat", None)
    in_specs = (field, field, plane, plane, plane, field, field, field, fresh, fresh, fresh)
    return jax.shard_map(
        functools.partial(body, mesh.shape["tm"], mesh.shape["lat"]),
        mesh=mesh,
        in_specs=in_specs,
        out_specs=(field, field),
        check_vma=False,
    )
```
